32 devices in a mesh: grp: 2 (over y), seq: 4 (over z), usr: 4 (over x, core).
Axes of the slice: x: 2, y: 2, z: 4, core: 2. Of those that a mesh axis runs over, the one named last changes fastest.
Arguments:
- history_kv: bfloat16 [16, 2048, 768], P(('grp', 'usr'), 'seq'), parts along dimension 0, may hold values from -6 to 6
- candidates: bfloat16 [16, 512, 768], P(('grp', 'usr'), 'seq'), parts along dimension 0, may hold values from -6 to 6
- lengths: int32 [16], P(('grp', 'usr')), parts along dimension 0, may hold values from 256 to 2048, as said below
- w_query: bfloat16 [768, 384], replicated, may hold values from -0.21875 to 0.21875
- w_gate: bfloat16 [768, 384], replicated, may hold values from -0.21875 to 0.21875
- token_mix: bfloat16 [512, 512], P('seq'), may hold values from -0.25 to 0.25
- w_out: bfloat16 [384, 768], replicated, may hold values from -0.3125 to 0.3125
- w_up: bfloat16 [768, 2048], P(None, 'usr'), may hold values from -0.21875 to 0.21875
- w_down: bfloat16 [2048, 768], P('usr'), may hold values from -0.125 to 0.125
Outputs:
- ranked: bfloat16 [16, 512, 768], P(('grp', 'usr'), 'seq'), parts along dimension 0
The draws below stay inside these ranges and needn't reach their ends.
There are 2 independent parts, one for each index of `grp`. The reference program is written for one: setup_inputs(seed, part) draws one part's arguments, and reference() takes and returns one part's arrays. A program takes and returns all parts, laid end to end along the dimension named above; an argument that names none is the same for every part. Nothing has to cross between parts.
Inputs may be any that keep to these rules, and one draw needn't show every extreme that they name: lengths[u] counts the first valid slots of user u's history; in every draw one user has exactly 2048 and another exactly 256.
All inputs are finite; a program needn't handle non-finite values.
Results may differ from the reference program's by a relative error of at most 0.008.
Values may be sent and summed in bfloat16 or wider, within the bound.
No kernel may reach another device: no remote copies, remote signals or barrier semaphores. Data moves between devices by JAX's collectives and lax.ppermute only.
A program may use at most 64 MiB of HBM per device.

```python
import math
import jax
import jax.numpy as jnp
from jax import lax

D = 768
HEADS = 3
DH = 128
FF = 2048
CANDS = 512
INNER = 384
USERS = 8
HIST = 2048


def draw_lengths(key, part):
    keys = jax.random.split(key, 2)
    drawn = jax.random.randint(keys[0], (USERS,), HIST // 8, HIST + 1, dtype=jnp.int32)
    order = jax.random.permutation(keys[1], jnp.arange(USERS, dtype=jnp.int32))
    positions = jnp.arange(USERS, dtype=jnp.int32)
    drawn = jnp.where(positions == order[0], HIST, drawn)
    drawn = jnp.where(positions == order[1], HIST // 8, drawn)
    return drawn.astype(jnp.int32)


def level_of(rng, extent, shards, low, top_value):
    level = 1.0
    for position, parts in shards:
        heights = jax.random.uniform(jax.random.fold_in(jax.random.fold_in(rng, 6), position), (parts,), jnp.float32, low / len(shards), top_value / len(shards))
        level = level * jnp.repeat(jnp.exp(heights), extent[position] // parts).reshape((-1,) + (1,) * (len(extent) - 1 - position))
    return level


def normal_values(key, dims, deviation, bound, shards=(), held_as=jnp.bfloat16):
    factor_of = level_of(key, dims, shards, -0.22, 0.18) if shards else 1.0
    values = jax.random.normal(key, dims, jnp.float32) * deviation * factor_of
    return jnp.minimum(jnp.maximum(values, -bound), bound).astype(held_as)


def setup_inputs(seed: int = 0, part: int = 0) -> dict:
    key_of = jax.random.split(jax.random.key(seed), 10)
    part_keys = jax.random.split(jax.random.fold_in(key_of[9], part), 10)
    history_kv = normal_values(part_keys[0], (USERS, HIST, 2 * INNER), 1.0, 6.0, ((0, 4), (1, 4)))
    candidates = normal_values(part_keys[1], (USERS, CANDS, D), 1.0, 6.0, ((0, 4), (1, 4)))
    lengths = draw_lengths(jax.random.fold_in(jax.random.fold_in(key_of[9], part), 71), part)
    w_query = normal_values(key_of[3], (D, INNER), D ** -0.5, 0.21875)
    w_gate = normal_values(key_of[4], (D, INNER), D ** -0.5, 0.21875)
    token_mix = normal_values(key_of[5], (CANDS, CANDS), CANDS ** -0.5, 0.25, ((0, 4),))
    w_out = normal_values(key_of[6], (INNER, D), INNER ** -0.5, 0.3125)
    w_up = normal_values(key_of[7], (D, FF), D ** -0.5, 0.21875, ((1, 4),))
    w_down = normal_values(key_of[8], (FF, D), FF ** -0.5, 0.125, ((0, 4),))
    return dict(history_kv=history_kv, candidates=candidates, lengths=lengths, w_query=w_query, w_gate=w_gate, token_mix=token_mix, w_out=w_out, w_up=w_up, w_down=w_down)


def rounded(values):
    return lax.optimization_barrier(values.astype(jnp.bfloat16)).astype(jnp.float32)

def layer_norm(values):
    center = values - lax.optimization_barrier(jnp.mean(values, axis=-1, keepdims=True))
    spread = lax.optimization_barrier(jnp.mean(center * center, axis=-1, keepdims=True))
    return center * lax.rsqrt(spread + 1e-05)

def reference(history_kv, candidates, lengths, w_query, w_gate, token_mix, w_out, w_up, w_down):
    inner = HEADS * DH
    scale = 1.0 / math.sqrt(DH)
    cand_f = candidates.astype(jnp.float32)
    queries = rounded(jnp.einsum('ucd,de->uce', cand_f, w_query.astype(jnp.float32)))
    block_len = math.gcd(HIST, 2048)
    block_count = HIST // block_len

    def one_user(operands):
        query_rows, cache, limit = operands
        query_heads = query_rows.reshape(CANDS, HEADS, DH)
        blocks = cache.reshape(block_count, block_len, 2 * inner)
        starts = jnp.arange(block_count, dtype=jnp.int32) * block_len

        def step(summed, item):
            block, start = item
            key_heads = block[:, :inner].astype(jnp.float32).reshape(block_len, HEADS, DH)
            value_heads = block[:, inner:].astype(jnp.float32).reshape(block_len, HEADS, DH)
            scores = jnp.einsum('chd,thd->hct', query_heads, key_heads) * scale
            positions = start + jnp.arange(block_len, dtype=jnp.int32)
            visible = positions < limit
            weights = rounded(jnp.where(visible[None, None, :], jax.nn.silu(scores), 0.0))
            contrib = jnp.einsum('hct,thd->chd', weights, value_heads).reshape(CANDS, inner)
            return (summed + contrib, None)
        summed, _ = lax.scan(step, jnp.zeros((CANDS, inner), jnp.float32), (blocks, starts))
        return summed
    attended = lax.map(one_user, (queries, history_kv, lengths))
    normed = rounded(layer_norm(attended))
    mixed = normed + jnp.einsum('cp,upe->uce', token_mix.astype(jnp.float32), normed)
    gate_values = jax.nn.silu(jnp.einsum('ucd,de->uce', cand_f, w_gate.astype(jnp.float32)))
    gated = rounded(mixed * gate_values)
    state = cand_f + jnp.einsum('uce,ed->ucd', gated, w_out.astype(jnp.float32))
    ffn_in = rounded(layer_norm(state))
    hidden = rounded(jax.nn.gelu(jnp.einsum('ucd,df->ucf', ffn_in, w_up.astype(jnp.float32))))
    ranked = state + jnp.einsum('ucf,fd->ucd', hidden, w_down.astype(jnp.float32))
    return ranked.astype(jnp.bfloat16)
```

```python
import functools
import math

import jax
import jax.numpy as jnp
from jax import lax
from jax.experimental import pallas as pl
from jax.experimental.pallas import tpu as pltpu
from jax.sharding import PartitionSpec as P

HEADS = 3
DH = 128
EPS = 1e-05
F32 = jnp.float32
BF16 = jnp.bfloat16
DIRECT_MAX = 8
VMEM = pl.BlockSpec(memory_space=pltpu.VMEM)
SMEM = pl.BlockSpec(memory_space=pltpu.SMEM)


def layer_norm(values):
    center = values - jnp.mean(values, axis=-1, keepdims=True)
    spread = jnp.mean(center * center, axis=-1, keepdims=True)
    return center * lax.rsqrt(spread + EPS)


def silu(values):
    half = 0.5 * values
    return half + half * jnp.tanh(half)


def params(mib):
    return pltpu.CompilerParams(vmem_limit_bytes=mib * 1024 * 1024)


def attention_kernel(count, group, info_ref, *refs):
    chunks, (kv_ref, out_ref, q_ref, v_ref) = refs[:count], refs[count:]
    rows = chunks[0].shape[1]
    slots, inner = kv_ref.shape[1], kv_ref.shape[2] // 2
    half_scale = 0.5 / math.sqrt(DH)
    total = q_ref.shape[0]
    block = math.gcd(total, 256)
    for member in range(group):
        for j, chunk in enumerate(chunks):
            start = pl.multiple_of(info_ref[1 + j] * rows, rows)
            q_ref[pl.ds(start, rows), :] = chunk[member]
        limit = info_ref[1 + count + member]
        valid = lax.broadcasted_iota(jnp.int32, (slots, inner), 0) < limit
        v_ref[...] = jnp.where(valid, kv_ref[member, :, inner:], jnp.zeros((), BF16))
        for head in range(inner // DH):
            cols = pl.ds(head * DH, DH)
            keys = kv_ref[member, :, cols]
            values = v_ref[:, cols]
            for r in range(0, total, block):
                scores = lax.dot_general(
                    q_ref[pl.ds(r, block), cols],
                    keys,
                    (((1,), (1,)), ((), ())),
                    preferred_element_type=F32,
                )
                half = scores * half_scale
                weights = (half + half * jnp.tanh(half)).astype(BF16)
                out_ref[member, pl.ds(r, block), cols] = jnp.dot(
                    weights, values, preferred_element_type=F32
                ).astype(BF16)


def attention(chunks, history_kv, info, group):
    count = len(chunks)
    _, rows, inner = chunks[0].shape
    slots, width = history_kv.shape[1:]
    total = rows * count

    def pick(i, info_ref):
        return (info_ref[0], 0, 0)

    spec = pltpu.PrefetchScalarGridSpec(
        num_scalar_prefetch=1,
        grid=(1,),
        in_specs=[pl.BlockSpec((group, rows, inner), pick)] * count
        + [pl.BlockSpec((group, slots, width), pick)],
        out_specs=pl.BlockSpec((group, total, inner), lambda i, info_ref: (0, 0, 0)),
        scratch_shapes=[pltpu.VMEM((total, inner), BF16), pltpu.VMEM((slots, inner), BF16)],
    )
    work = group * total * slots * inner
    return pl.pallas_call(
        functools.partial(attention_kernel, count, group),
        grid_spec=spec,
        out_shape=jax.ShapeDtypeStruct((group, total, inner), BF16),
        compiler_params=params(24),
        cost_estimate=pl.CostEstimate(
            flops=4 * work, bytes_accessed=2 * group * (slots * width + 2 * total * inner), transcendentals=work // DH
        ),
    )(info, *chunks, history_kv)


def mix_kernel(sums, blocks, *refs):
    parts, mixes = refs[:sums], refs[sums : sums + blocks]
    pos_ref, outs = refs[sums + blocks], refs[sums + blocks + 1 : sums + 2 * blocks + 1]
    normed_ref = refs[-1]
    rows = outs[0].shape[1]
    for member in range(parts[0].shape[0]):
        attended = parts[0][member].astype(F32)
        for part in parts[1:]:
            attended = attended + part[member].astype(F32)
        normed_ref[...] = layer_norm(attended).astype(BF16)
        for j in range(blocks):
            start = pl.multiple_of(pos_ref[j] * rows, rows)
            own = normed_ref[pl.ds(start, rows), :].astype(F32)
            mixed = own + jnp.dot(mixes[j][...], normed_ref[...], preferred_element_type=F32)
            outs[j][member] = mixed.astype(BF16)


def mix(parts, mixes, positions):
    group, total, inner = parts[0].shape
    rows = mixes[0].shape[0]
    blocks = len(mixes)
    return pl.pallas_call(
        functools.partial(mix_kernel, len(parts), blocks),
        in_specs=[VMEM] * (len(parts) + blocks) + [SMEM],
        out_specs=[VMEM] * blocks,
        out_shape=[jax.ShapeDtypeStruct((group, rows, inner), BF16)] * blocks,
        scratch_shapes=[pltpu.VMEM((total, inner), BF16)],
        compiler_params=params(24),
        cost_estimate=pl.CostEstimate(
            flops=2 * group * total * inner * rows * blocks,
            bytes_accessed=2 * total * (group * inner * (len(parts) + 1) + total),
            transcendentals=total,
        ),
    )(*parts, *mixes, positions)


def tail_kernel(shares, mixed_ref, gate_ref, cand_ref, w_out_ref, *refs):
    ups, downs, out_ref = refs[:shares], refs[shares : 2 * shares], refs[2 * shares]
    gated = (mixed_ref[...].astype(F32) * gate_ref[...].astype(F32)).astype(BF16)
    state = cand_ref[...].astype(F32) + jnp.dot(gated, w_out_ref[...], preferred_element_type=F32)
    ffn_in = layer_norm(state).astype(BF16)
    total = state
    for up, down in zip(ups, downs):
        hidden = jax.nn.gelu(jnp.dot(ffn_in, up[...], preferred_element_type=F32)).astype(BF16)
        total = total + jnp.dot(hidden, down[...], preferred_element_type=F32)
    out_ref[...] = total.astype(BF16)


def tail(mixed, gate, candidates, w_out, ups, downs):
    rows, inner = mixed.shape
    width = candidates.shape[1]
    hidden = sum(up.shape[1] for up in ups)
    return pl.pallas_call(
        functools.partial(tail_kernel, len(ups)),
        in_specs=[VMEM] * (4 + 2 * len(ups)),
        out_specs=VMEM,
        out_shape=jax.ShapeDtypeStruct((rows, width), BF16),
        compiler_params=params(32),
        cost_estimate=pl.CostEstimate(
            flops=2 * rows * width * (inner + 2 * hidden),
            bytes_accessed=2 * width * (2 * hidden + inner + 2 * rows),
            transcendentals=rows * hidden,
        ),
    )(mixed, gate, candidates, w_out, *ups, *downs)


def doubling(arrays, axis, count):
    held = [[array] for array in arrays]
    step = count // 2
    while step:
        pairs = [(i, i ^ step) for i in range(count)]
        held = [own + [lax.ppermute(a, axis, pairs) for a in own] for own in held]
        step //= 2
    return held


def gather_shares(w_up, w_down, count):
    if count & (count - 1) == 0:
        return doubling((w_up, w_down), "usr", count)
    ups = lax.all_gather(w_up, "usr")
    downs = lax.all_gather(w_down, "usr")
    return [ups[i] for i in range(count)], [downs[i] for i in range(count)]


def middle_pairs(count):
    left, right = count // 2 - 1, count // 2
    near = [[(left - d, left), (right + d, right)] for d in range(1, count // 2)]
    far = [[(left - d, right), (right + d, left)] for d in range(count // 2)]
    return near, far


def reverse(pairs):
    return [(b, a) for a, b in pairs]


def mixed_direct(queries, history_kv, lengths, token_mix, count, usr_count):
    users = queries.shape[0]
    group = users // 2
    slots = history_kv.shape[1]
    seq = lax.axis_index("seq").astype(jnp.int32)
    left, right = count // 2 - 1, count // 2
    near, far = middle_pairs(count)
    on_right = (seq >= right).astype(jnp.int32)

    chunks = [queries]
    places = [seq]
    for k in range(count - 1, 0, -1):
        chunks.append(lax.ppermute(queries, "seq", [(i, i ^ k) for i in range(count)]))
        places.append(seq ^ k)

    pairs_usr = [(i, i ^ 1) for i in range(usr_count)]
    split = usr_count % 2 == 0 and token_mix.shape[0] % 32 == 0
    piece = token_mix
    if split:
        piece_rows = token_mix.shape[0] // 2
        odd = lax.axis_index("usr") % 2
        piece = lax.dynamic_slice_in_dim(token_mix, odd * piece_rows, piece_rows, 0)
    pieces = [lax.ppermute(piece, "seq", pairs) for pairs in near + far]
    if split:
        stack = jnp.stack(pieces)
        other = lax.ppermute(stack, "usr", pairs_usr)
        low = jnp.where(odd == 0, stack, other)
        high = jnp.where(odd == 0, other, stack)
        both = jnp.concatenate([low, high], axis=1)
        pieces = [both[i] for i in range(len(pieces))]
    mixes = [token_mix] + pieces
    steps = [-d for d in range(1, count // 2)] + [d + 1 for d in range(count // 2)]
    positions = jnp.stack(
        [seq] + [jnp.clip(jnp.where(on_right == 1, seq - s, seq + s), 0, count - 1) for s in steps]
    ).astype(jnp.int32)

    valid = jnp.clip(lengths - seq * slots, 0, slots).reshape(2, group)

    def sums(which):
        info = jnp.concatenate([jnp.stack([which] + places), valid[which]]).astype(jnp.int32)
        return attention(chunks, history_kv, info, group)

    far_sums = sums(1 - on_right)
    far_parts = [lax.ppermute(far_sums, "seq", pairs) for pairs in far]
    near_sums = sums(on_right)
    near_parts = [lax.ppermute(near_sums, "seq", pairs) for pairs in near]

    outs = mix([near_sums] + near_parts + far_parts, mixes, positions)
    own, outs = outs[0], outs[1:]
    back = [lax.ppermute(o, "seq", reverse(pairs)) for o, pairs in zip(outs, near + far)]
    is_middle = (seq == left) | (seq == right)
    near_mixed = own
    if near:
        near_mixed = jnp.where(is_middle, own, functools.reduce(jnp.add, back[: len(near)]))
    far_mixed = functools.reduce(jnp.add, back[len(near) :])
    low = jnp.where(on_right == 1, far_mixed, near_mixed)
    high = jnp.where(on_right == 1, near_mixed, far_mixed)
    return jnp.concatenate([low, high], axis=0)


def mixed_scattered(queries, history_kv, lengths, token_mix):
    users = queries.shape[0]
    slots = history_kv.shape[1]
    seq = lax.axis_index("seq").astype(jnp.int32)
    gathered = lax.all_gather(queries, "seq", axis=1, tiled=True)
    valid = jnp.clip(lengths - seq * slots, 0, slots)
    info = jnp.concatenate([jnp.zeros((2,), jnp.int32), valid]).astype(jnp.int32)
    sums = attention([gathered], history_kv, info, users)
    attended = lax.psum_scatter(sums.astype(F32), "seq", scatter_dimension=1, tiled=True)
    normed = layer_norm(attended).astype(BF16)
    everyone = lax.all_gather(normed, "seq", axis=1, tiled=True)
    mixed = normed.astype(F32) + jnp.einsum("cp,upe->uce", token_mix, everyone, preferred_element_type=F32)
    return mixed.astype(BF16)


def shards(seq_count, usr_count, history_kv, candidates, lengths, w_query, w_gate, token_mix, w_out, w_up, w_down):
    users, rows, width = candidates.shape
    inner = w_query.shape[1]
    flat = candidates.reshape(users * rows, width)
    queries = jnp.dot(flat, w_query, preferred_element_type=F32).astype(BF16).reshape(users, rows, inner)
    direct = seq_count & (seq_count - 1) == 0 and 2 <= seq_count <= DIRECT_MAX and users % 2 == 0
    if direct:
        mixed = mixed_direct(queries, history_kv, lengths, token_mix, seq_count, usr_count)
    else:
        mixed = mixed_scattered(queries, history_kv, lengths, token_mix)
    ups, downs = gather_shares(w_up, w_down, usr_count)
    gate = silu(jnp.dot(flat, w_gate, preferred_element_type=F32))
    ranked = tail(mixed.reshape(users * rows, inner), gate, flat, w_out, ups, downs)
    return ranked.reshape(users, rows, width)


def solution(mesh):
    return jax.shard_map(
        functools.partial(shards, mesh.shape["seq"], mesh.shape["usr"]),
        mesh=mesh,
        in_specs=(
            P(("grp", "usr"), "seq", None),
            P(("grp", "usr"), "seq", None),
            P(("grp", "usr")),
            P(),
            P(),
            P("seq", None),
            P(),
            P(None, "usr"),
            P("usr", None),
        ),
        out_specs=P(("grp", "usr"), "seq", None),
        check_vma=False,
    )
```

```python
import functools
import math

import jax
import jax.numpy as jnp
from jax import lax
from jax.experimental import pallas as pl
from jax.experimental.pallas import tpu as pltpu
from jax.sharding import PartitionSpec as P

HEADS = 3
DH = 128
EPS = 1e-05
F32 = jnp.float32
BF16 = jnp.bfloat16
DIRECT_MAX = 8
VMEM = pl.BlockSpec(memory_space=pltpu.VMEM)
SMEM = pl.BlockSpec(memory_space=pltpu.SMEM)


def layer_norm(values):
    center = values - jnp.mean(values, axis=-1, keepdims=True)
    spread = jnp.mean(center * center, axis=-1, keepdims=True)
    return center * lax.rsqrt(spread + EPS)


def silu(values):
    half = 0.5 * values
    return half + half * jnp.tanh(half)


def params(mib):
    return pltpu.CompilerParams(vmem_limit_bytes=mib * 1024 * 1024)


def attention_kernel(places, halves, right, seq_ref, lengths_ref, *refs):
    count = len(places)
    chunks, kv_ref = refs[:count], refs[count]
    outs, (q_ref, v_ref) = refs[-2 - halves : -2], refs[-2:]
    users, rows, inner = chunks[0].shape
    slots = kv_ref.shape[1]
    group = users // halves
    half_scale = 0.5 / math.sqrt(DH)
    seq = seq_ref[0]
    on_right = (seq >= right).astype(jnp.int32)
    total = rows * count
    block = math.gcd(total, 128)
    for which in range(halves):
        first = ((1 - on_right) if which == 0 else on_right) * group if halves == 2 else 0
        for member in range(group):
            user = first + member
            for j, chunk in enumerate(chunks):
                q_ref[j * rows : (j + 1) * rows, :] = chunk[user]
            limit = lengths_ref[user] - seq * slots
            valid = lax.broadcasted_iota(jnp.int32, (slots, inner), 0) < limit
            v_ref[...] = jnp.where(valid, kv_ref[user, :, inner:], jnp.zeros((), BF16))
            for head in range(inner // DH):
                cols = pl.ds(head * DH, DH)
                keys = kv_ref[user, :, cols]
                values = v_ref[:, cols]
                for r in range(0, total, block):
                    scores = lax.dot_general(
                        q_ref[r : r + block, cols],
                        keys,
                        (((1,), (1,)), ((), ())),
                        preferred_element_type=F32,
                    )
                    half = scores * half_scale
                    weights = (half + half * jnp.tanh(half)).astype(BF16)
                    sums = jnp.dot(weights, values, preferred_element_type=F32).astype(BF16)
                    if count == 1 and places[0] is None:
                        outs[which][member, r : r + block, cols] = sums
                    else:
                        start = (seq ^ places[r // rows]) * rows + r % rows
                        outs[which][member, pl.ds(pl.multiple_of(start, block), block), cols] = sums


def attention(seq, lengths, chunks, places, history_kv, halves, right, total, into=None):
    count = len(chunks)
    users, rows, inner = chunks[0].shape
    slots, width = history_kv.shape[1:]
    work = users * rows * count * slots * inner
    ops = [seq, lengths, *chunks, history_kv] + (into or [])
    return pl.pallas_call(
        functools.partial(attention_kernel, places, halves, right),
        in_specs=[SMEM, SMEM] + [VMEM] * (count + 1) + ([VMEM] * halves if into else []),
        out_specs=[VMEM] * halves,
        out_shape=[jax.ShapeDtypeStruct((users // halves, total, inner), BF16)] * halves,
        input_output_aliases={3 + count + i: i for i in range(halves)} if into else {},
        scratch_shapes=[pltpu.VMEM((rows * count, inner), BF16), pltpu.VMEM((slots, inner), BF16)],
        compiler_params=params(16),
        cost_estimate=pl.CostEstimate(
            flops=4 * work, bytes_accessed=2 * users * (slots * width + 2 * rows * count * inner), transcendentals=work // DH
        ),
    )(*ops)


def mix_kernel(sums, right, steps, *refs):
    seq_ref, part_ref = refs[:2]
    parts, (mine_ref, other_ref) = refs[2 : 2 + sums], refs[2 + sums : 4 + sums]
    outs, (normed_ref, mix_ref) = refs[4 + sums : -2], refs[-2:]
    blocks, share, total = mine_ref.shape
    rows = total // blocks
    seq, part = seq_ref[0], part_ref[0]
    on_right = seq >= right
    for j in range(blocks):
        mix_ref[pl.ds(pl.multiple_of(j * rows + part * share, share), share), :] = mine_ref[j]
        if share < rows:
            mix_ref[pl.ds(pl.multiple_of(j * rows + (1 - part) * share, share), share), :] = other_ref[j]
    for member in range(parts[0].shape[0]):
        attended = parts[0][member].astype(F32)
        for p in parts[1:]:
            attended = attended + p[member].astype(F32)
        normed_ref[...] = layer_norm(attended).astype(BF16)
        for j in range(blocks):
            place = jnp.clip(jnp.where(on_right, seq - steps[j], seq + steps[j]), 0, blocks - 1)
            own = normed_ref[pl.ds(pl.multiple_of(place * rows, rows), rows), :].astype(F32)
            mixed = own + jnp.dot(
                mix_ref[j * rows : (j + 1) * rows, :], normed_ref[...], preferred_element_type=F32
            )
            outs[j][member] = mixed.astype(BF16)


def mix(seq, part, parts, mine, other, right, steps):
    group, total, inner = parts[0].shape
    blocks = len(steps)
    rows = total // blocks
    return pl.pallas_call(
        functools.partial(mix_kernel, len(parts), right, steps),
        in_specs=[SMEM, SMEM] + [VMEM] * (len(parts) + 2),
        out_specs=[VMEM] * blocks,
        out_shape=[jax.ShapeDtypeStruct((group, rows, inner), BF16)] * blocks,
        scratch_shapes=[pltpu.VMEM((total, inner), BF16), pltpu.VMEM((total, total), BF16)],
        compiler_params=params(12),
        cost_estimate=pl.CostEstimate(
            flops=2 * group * total * inner * rows * blocks,
            bytes_accessed=2 * total * (group * inner * (len(parts) + 1) + total),
            transcendentals=total,
        ),
    )(seq, part, *parts, mine, other)


def tail_kernel(shares, nears, fars, left, hidden, seq_ref, *refs):
    pieces, refs = refs[: 1 + nears + fars], refs[1 + nears + fars :]
    cand_ref, w_gate_ref, w_out_ref = refs[:3]
    packs, (out_ref, mixed_ref) = refs[3 : 3 + shares], refs[3 + shares :]
    users, rows, width = cand_ref.shape
    inner = w_gate_ref.shape[1]
    own = pieces[0]
    if fars == 0:
        mixed_ref[...] = own[...]
    else:
        group = own.shape[0]
        seq = seq_ref[0]
        on_right = (seq > left).astype(jnp.int32)
        middle = (seq == left) | (seq == left + 1)
        for member in range(group):
            near_rows = own[member]
            if nears:
                came = functools.reduce(jnp.add, [p[member] for p in pieces[1 : 1 + nears]])
                near_rows = jnp.where(middle, near_rows, came)
            mixed_ref[on_right * group + member] = near_rows
            far_rows = functools.reduce(jnp.add, [p[member] for p in pieces[1 + nears :]])
            mixed_ref[(1 - on_right) * group + member] = far_rows
    cand = cand_ref[...].reshape(users * rows, width)
    gate = silu(jnp.dot(cand, w_gate_ref[...], preferred_element_type=F32))
    gated = (mixed_ref[...].reshape(users * rows, inner).astype(F32) * gate).astype(BF16)
    state = cand.astype(F32) + jnp.dot(gated, w_out_ref[...], preferred_element_type=F32)
    ffn_in = layer_norm(state).astype(BF16)
    deep = packs[0].shape[1]
    ups = hidden // deep
    terms = [state[:, d : d + deep] for d in range(0, width, deep)]
    for pack in packs:
        values = [
            jax.nn.gelu(jnp.dot(ffn_in, pack[j * width : (j + 1) * width, :], preferred_element_type=F32)).astype(BF16)
            for j in range(ups)
        ]
        values = jnp.concatenate(values, axis=1)
        for d in range(width // deep):
            start = ups * width + d * hidden
            terms[d] = terms[d] + jnp.dot(values, pack[start : start + hidden, :], preferred_element_type=F32)
    total = jnp.concatenate(terms, axis=1)
    out_ref[...] = total.astype(BF16).reshape(users, rows, width)


def tail(seq, pieces, nears, fars, left, candidates, w_gate, w_out, packs, hidden):
    users, rows, width = candidates.shape
    inner = w_gate.shape[1]
    total = users * rows
    return pl.pallas_call(
        functools.partial(tail_kernel, len(packs), nears, fars, left, hidden),
        in_specs=[SMEM] + [VMEM] * (len(pieces) + 3 + len(packs)),
        out_specs=VMEM,
        out_shape=jax.ShapeDtypeStruct((users, rows, width), BF16),
        scratch_shapes=[pltpu.VMEM((users, rows, inner), BF16)],
        compiler_params=params(24),
        cost_estimate=pl.CostEstimate(
            flops=2 * total * width * (2 * inner + 2 * hidden * len(packs)),
            bytes_accessed=2 * width * (2 * hidden * len(packs) + inner + 2 * total),
            transcendentals=total * hidden * len(packs),
        ),
    )(seq, *pieces, candidates, w_gate, w_out, *packs)


def packed(w_up, w_down):
    deep = math.gcd(w_up.shape[1], w_down.shape[1])
    return jnp.concatenate([w[:, c : c + deep] for w in (w_up, w_down) for c in range(0, w.shape[1], deep)], axis=0)


def gather_shares(pack, count, early, late):
    if count & (count - 1):
        everyone = lax.all_gather(pack, "usr")
        return [everyone[i] for i in range(count)]
    held = [pack]
    step = count // 2
    while step:
        pairs = [(i, i ^ step) for i in range(count)]
        if len(held) > 1:
            held = [after(held[0], early)] + [after(a, late) for a in held[1:]]
        held = held + [lax.ppermute(a, "usr", pairs) for a in held]
        step //= 2
    return held


def middle_pairs(count):
    left, right = count // 2 - 1, count // 2
    near = [[(left - d, left), (right + d, right)] for d in range(1, count // 2)]
    far = [[(left - d, right), (right + d, left)] for d in range(count // 2)]
    return near, far


def reverse(pairs):
    return [(b, a) for a, b in pairs]


def after(value, other):
    return lax.optimization_barrier((value, other))[0]


def mixed_direct(seq, queries, history_kv, lengths, token_mix, count, usr_count):
    left, right = count // 2 - 1, count // 2
    near, far = middle_pairs(count)
    total = queries.shape[1] * count
    place = lax.axis_index("usr").astype(jnp.int32)

    blocks, places = [queries], [0]
    step = count // 2
    first = None
    while step:
        pairs = [(i, i ^ step) for i in range(count)]
        came = [lax.ppermute(b, "seq", pairs) for b in blocks]
        first = came[0] if first is None else first
        blocks, places = blocks + came, places + [p ^ step for p in places]
        step //= 2

    split = usr_count % 2 == 0 and token_mix.shape[0] % 32 == 0
    part = (place % 2 if split else jnp.zeros((), jnp.int32)).reshape(1)
    piece = after(token_mix, queries)
    if split:
        piece_rows = token_mix.shape[0] // 2
        piece = lax.dynamic_slice_in_dim(piece, part[0] * piece_rows, piece_rows, 0)
    mine = jnp.stack([piece] + [lax.ppermute(piece, "seq", pairs) for pairs in near])
    mine = jnp.concatenate([mine, lax.ppermute(after(mine, first), "seq", far[0])])
    other = lax.ppermute(mine, "usr", [(i, i ^ 1) for i in range(usr_count)]) if split else mine
    steps = [0] + [-d for d in range(1, count // 2)] + [d + 1 for d in range(count // 2)]

    early = len(blocks) - len(blocks) // 4 if len(blocks) >= 4 else len(blocks)
    sums = attention(seq, lengths, blocks[:early], places[:early], history_kv, 2, right, total)
    if early < len(blocks):
        sums = attention(seq, lengths, blocks[early:], places[early:], history_kv, 2, right, total, list(sums))
    far_sums, near_sums = sums
    far_parts = [lax.ppermute(far_sums, "seq", pairs) for pairs in reversed(far)]
    near_parts = [lax.ppermute(near_sums, "seq", pairs) for pairs in near]

    outs = mix(seq, part, [near_sums] + near_parts + far_parts, mine, other, right, steps)
    back = [lax.ppermute(o, "seq", reverse(pairs)) for o, pairs in zip(outs[1:], near + far)]
    return [outs[0]] + back, len(near), len(far), first, outs[0]


def mixed_scattered(seq, queries, history_kv, lengths, token_mix):
    gathered = lax.all_gather(queries, "seq", axis=1, tiled=True)
    sums = attention(seq, lengths, [gathered], [None], history_kv, 1, 0, gathered.shape[1])[0]
    attended = lax.psum_scatter(sums.astype(F32), "seq", scatter_dimension=1, tiled=True)
    normed = layer_norm(attended).astype(BF16)
    everyone = lax.all_gather(normed, "seq", axis=1, tiled=True)
    mixed = normed.astype(F32) + jnp.einsum("cp,upe->uce", token_mix, everyone, preferred_element_type=F32)
    return [mixed.astype(BF16)], 0, 0, gathered, sums


def shards(seq_count, usr_count, history_kv, candidates, lengths, w_query, w_gate, token_mix, w_out, w_up, w_down):
    users, rows, width = candidates.shape
    inner = w_query.shape[1]
    seq = lax.axis_index("seq").astype(jnp.int32).reshape(1)
    flat = candidates.reshape(users * rows, width)
    queries = jnp.dot(flat, w_query, preferred_element_type=F32).astype(BF16).reshape(users, rows, inner)
    direct = seq_count & (seq_count - 1) == 0 and 2 <= seq_count <= DIRECT_MAX and users % 2 == 0
    if direct:
        pieces, nears, fars, early, late = mixed_direct(seq, queries, history_kv, lengths, token_mix, seq_count, usr_count)
    else:
        pieces, nears, fars, early, late = mixed_scattered(seq, queries, history_kv, lengths, token_mix)
    packs = gather_shares(packed(*after((w_up, w_down), queries)), usr_count, early, late)
    return tail(seq, pieces, nears, fars, seq_count // 2 - 1, candidates, w_gate, w_out, packs, w_up.shape[1])


def solution(mesh):
    return jax.shard_map(
        functools.partial(shards, mesh.shape["seq"], mesh.shape["usr"]),
        mesh=mesh,
        in_specs=(
            P(("grp", "usr"), "seq", None),
            P(("grp", "usr"), "seq", None),
            P(("grp", "usr")),
            P(),
            P(),
            P("seq", None),
            P(),
            P(None, "usr"),
            P("usr", None),
        ),
        out_specs=P(("grp", "usr"), "seq", None),
        check_vma=False,
    )
```

```python
import functools
import math

import jax
import jax.numpy as jnp
from jax import lax
from jax.experimental import pallas as pl
from jax.experimental.pallas import tpu as pltpu
from jax.sharding import PartitionSpec as P

HEADS = 3
DH = 128
EPS = 1e-05
F32 = jnp.float32
BF16 = jnp.bfloat16
DIRECT_MAX = 8
WEIGHT = 10
VMEM = pl.BlockSpec(memory_space=pltpu.VMEM)
SMEM = pl.BlockSpec(memory_space=pltpu.SMEM)


def layer_norm(values):
    center = values - jnp.mean(values, axis=-1, keepdims=True)
    spread = jnp.mean(center * center, axis=-1, keepdims=True)
    return center * lax.rsqrt(spread + EPS)


def silu(values):
    half = 0.5 * values
    return half + half * jnp.tanh(half)


def params(mib):
    return pltpu.CompilerParams(vmem_limit_bytes=mib * 1024 * 1024)


def attention_kernel(places, sides, right, seq_ref, lengths_ref, *refs):
    count = len(places)
    chunks, kv_ref = refs[:count], refs[count]
    outs, (q_ref, v_ref) = refs[-2 - len(sides) : -2], refs[-2:]
    _, rows, inner = chunks[0].shape
    slots = kv_ref.shape[1]
    half_scale = 0.5 / math.sqrt(DH)
    seq = seq_ref[0]
    on_right = (seq >= right).astype(jnp.int32)
    total = rows * count
    block = math.gcd(total, 128)
    for out_ref, side in zip(outs, sides):
        group = out_ref.shape[0]
        first = 0 if side is None else (on_right ^ side) * group
        for member in range(group):
            user = first + member
            for j, chunk in enumerate(chunks):
                q_ref[j * rows : (j + 1) * rows, :] = chunk[user]
            limit = lengths_ref[user] - seq * slots
            valid = lax.broadcasted_iota(jnp.int32, (slots, inner), 0) < limit
            v_ref[...] = jnp.where(valid, kv_ref[user, :, inner:], jnp.zeros((), BF16))
            for head in range(inner // DH):
                cols = pl.ds(head * DH, DH)
                keys = kv_ref[user, :, cols]
                values = v_ref[:, cols]
                for r in range(0, total, block):
                    scores = lax.dot_general(
                        q_ref[r : r + block, cols],
                        keys,
                        (((1,), (1,)), ((), ())),
                        preferred_element_type=F32,
                    )
                    half = scores * half_scale
                    weights = (half + half * jnp.tanh(half)).astype(BF16)
                    sums = jnp.dot(weights, values, preferred_element_type=F32).astype(BF16)
                    if places[r // rows] is None:
                        out_ref[member, r : r + block, cols] = sums
                    else:
                        start = (seq ^ places[r // rows]) * rows + r % rows
                        out_ref[member, pl.ds(pl.multiple_of(start, block), block), cols] = sums


def attention(seq, lengths, chunks, places, history_kv, right, total, sides, into=()):
    count = len(chunks)
    users, rows, inner = chunks[0].shape
    slots, width = history_kv.shape[1:]
    group = users if sides[0] is None else users // 2
    work = group * len(sides) * rows * count * slots * inner
    return pl.pallas_call(
        functools.partial(attention_kernel, places, sides, right),
        in_specs=[SMEM, SMEM] + [VMEM] * (count + 1 + len(into)),
        out_specs=[VMEM] * len(sides),
        out_shape=[jax.ShapeDtypeStruct((group, total, inner), BF16)] * len(sides),
        input_output_aliases={3 + count + i: i for i in range(len(into))},
        scratch_shapes=[pltpu.VMEM((rows * count, inner), BF16), pltpu.VMEM((slots, inner), BF16)],
        compiler_params=params(16),
        cost_estimate=pl.CostEstimate(
            flops=WEIGHT * 4 * work, bytes_accessed=2 * users * (slots * width + 2 * rows * count * inner), transcendentals=work // DH
        ),
    )(seq, lengths, *chunks, history_kv, *into)


def normed_mix(seq_ref, part_ref, mine_ref, other_ref, normed_ref, mix_ref, member, right, step, j):
    blocks, share, total = mine_ref.shape
    rows = total // blocks
    seq, part = seq_ref[0], part_ref[0]
    mix_ref[pl.ds(pl.multiple_of(part * share, share), share), :] = mine_ref[j]
    if share < rows:
        mix_ref[pl.ds(pl.multiple_of((1 - part) * share, share), share), :] = other_ref[j]
    place = jnp.clip(jnp.where(seq >= right, seq - step, seq + step), 0, blocks - 1)
    own = normed_ref[member, pl.ds(pl.multiple_of(place * rows, rows), rows), :].astype(F32)
    return (own + jnp.dot(mix_ref[...], normed_ref[member], preferred_element_type=F32)).astype(BF16)


def far_mix_kernel(sums, right, steps, picked, *refs):
    seq_ref, part_ref = refs[:2]
    parts, (mine_ref, other_ref) = refs[2 : 2 + sums], refs[2 + sums : 4 + sums]
    normed_ref, outs, mix_ref = refs[4 + sums], refs[5 + sums : -1], refs[-1]
    for member in range(normed_ref.shape[0]):
        attended = parts[0][member].astype(F32)
        for p in parts[1:]:
            attended = attended + p[member].astype(F32)
        normed_ref[member] = layer_norm(attended).astype(BF16)
        for out_ref, j in zip(outs, picked):
            out_ref[member] = normed_mix(
                seq_ref, part_ref, mine_ref, other_ref, normed_ref, mix_ref, member, right, steps[j], j
            )


def near_mix_kernel(right, steps, picked, *refs):
    seq_ref, part_ref, normed_ref, mine_ref, other_ref = refs[:5]
    outs, mix_ref = refs[5:-1], refs[-1]
    for member in range(normed_ref.shape[0]):
        for out_ref, j in zip(outs, picked):
            out_ref[member] = normed_mix(
                seq_ref, part_ref, mine_ref, other_ref, normed_ref, mix_ref, member, right, steps[j], j
            )


def mix(seq, part, parts, mine, other, right, steps, picked, normed=None):
    group, total, inner = (normed if parts is None else parts[0]).shape
    rows = total // len(steps)
    block = jax.ShapeDtypeStruct((group, rows, inner), BF16)
    if parts is None:
        kernel = functools.partial(near_mix_kernel, right, steps, picked)
        ops, extra = [normed], []
    else:
        kernel = functools.partial(far_mix_kernel, len(parts), right, steps, picked)
        ops, extra = parts, [jax.ShapeDtypeStruct((group, total, inner), BF16)]
    shapes = extra + [block] * len(picked)
    return pl.pallas_call(
        kernel,
        in_specs=[SMEM, SMEM] + [VMEM] * (len(ops) + 2),
        out_specs=[VMEM] * len(shapes),
        out_shape=shapes,
        scratch_shapes=[pltpu.VMEM((rows, total), BF16)],
        compiler_params=params(12),
        cost_estimate=pl.CostEstimate(
            flops=2 * group * total * inner * rows * len(picked),
            bytes_accessed=2 * total * (group * inner * (len(ops) + 1) + total),
            transcendentals=total,
        ),
    )(seq, part, *ops, mine, other)


def tail_kernel(shares, nears, fars, left, seq_ref, *refs):
    pieces, refs = refs[: 1 + nears + fars], refs[1 + nears + fars :]
    cand_ref, w_gate_ref, w_out_ref = refs[:3]
    ups, downs = refs[3 : 3 + shares], refs[3 + shares : 3 + 2 * shares]
    out_ref, mixed_ref = refs[3 + 2 * shares :]
    users, rows, width = cand_ref.shape
    inner = w_gate_ref.shape[1]
    own = pieces[0]
    if fars == 0:
        mixed_ref[...] = own[...]
    else:
        group = own.shape[0]
        seq = seq_ref[0]
        on_right = (seq > left).astype(jnp.int32)
        middle = (seq == left) | (seq == left + 1)
        for member in range(group):
            near_rows = own[member]
            if nears:
                came = functools.reduce(jnp.add, [p[member] for p in pieces[1 : 1 + nears]])
                near_rows = jnp.where(middle, near_rows, came)
            mixed_ref[on_right * group + member] = near_rows
            far_rows = functools.reduce(jnp.add, [p[member] for p in pieces[1 + nears :]])
            mixed_ref[(1 - on_right) * group + member] = far_rows
    cand = cand_ref[...].reshape(users * rows, width)
    gate = silu(jnp.dot(cand, w_gate_ref[...], preferred_element_type=F32))
    gated = (mixed_ref[...].reshape(users * rows, inner).astype(F32) * gate).astype(BF16)
    state = cand.astype(F32) + jnp.dot(gated, w_out_ref[...], preferred_element_type=F32)
    ffn_in = layer_norm(state).astype(BF16)
    total = state
    for up, down in zip(ups, downs):
        hidden = jax.nn.gelu(jnp.dot(ffn_in, up[...], preferred_element_type=F32)).astype(BF16)
        total = total + jnp.dot(hidden, down[...], preferred_element_type=F32)
    out_ref[...] = total.astype(BF16).reshape(users, rows, width)


def tail(seq, pieces, nears, fars, left, candidates, w_gate, w_out, ups, downs):
    users, rows, width = candidates.shape
    inner = w_gate.shape[1]
    hidden = sum(up.shape[1] for up in ups)
    total = users * rows
    return pl.pallas_call(
        functools.partial(tail_kernel, len(ups), nears, fars, left),
        in_specs=[SMEM] + [VMEM] * (len(pieces) + 3 + 2 * len(ups)),
        out_specs=VMEM,
        out_shape=jax.ShapeDtypeStruct((users, rows, width), BF16),
        scratch_shapes=[pltpu.VMEM((users, rows, inner), BF16)],
        compiler_params=params(24),
        cost_estimate=pl.CostEstimate(
            flops=2 * total * width * (2 * inner + 2 * hidden),
            bytes_accessed=2 * width * (2 * hidden + inner + 2 * total),
            transcendentals=total * hidden,
        ),
    )(seq, *pieces, candidates, w_gate, w_out, *ups, *downs)


def narrow_exchanges(share, count):
    held = [share]
    step = count // 4
    while step:
        held = held + [lax.ppermute(a, "usr", [(i, i ^ step) for i in range(count)]) for a in held]
        step //= 2
    return held[1:]


def middle_pairs(count):
    left, right = count // 2 - 1, count // 2
    near = [[(left - d, left), (right + d, right)] for d in range(1, count // 2)]
    far = [[(left - d, right), (right + d, left)] for d in range(count // 2)]
    return near, far


def reverse(pairs):
    return [(b, a) for a, b in pairs]


def together(*values):
    return lax.optimization_barrier(values)


def mixed_direct(seq, queries, history_kv, lengths, token_mix, count, usr_count, held):
    left, right = count // 2 - 1, count // 2
    near, far = middle_pairs(count)
    total = queries.shape[1] * count
    place = lax.axis_index("usr").astype(jnp.int32)

    attend = functools.partial(attention, seq, lengths, history_kv=history_kv, right=right, total=total)
    split = usr_count % 2 == 0 and token_mix.shape[0] % 32 == 0
    part = (place % 2 if split else jnp.zeros((), jnp.int32)).reshape(1)
    blocks, places = [queries], [0]
    step = count // 2
    mine = None
    while step:
        if mine is not None and step == 1:
            mine, blocks[1] = together(mine, blocks[1])
        ends = [queries] + blocks[1:]
        came = [lax.ppermute(b, "seq", [(i, i ^ step) for i in range(count)]) for b in ends]
        if mine is None:
            sums = attend([queries], [0], sides=(1, 0))
            sums, piece = held(sums)
            if split:
                piece_rows = piece.shape[0] // 2
                piece = lax.dynamic_slice_in_dim(piece, part[0] * piece_rows, piece_rows, 0)
            mine = jnp.stack([piece] + [lax.ppermute(piece, "seq", pairs) for pairs in near])
        blocks = blocks + came
        places = places + [p ^ step for p in places]
        step //= 2
    steps = [0] + [-d for d in range(1, count // 2)] + [d + 1 for d in range(count // 2)]

    crossed = lax.ppermute(mine, "seq", far[0])
    begin = max(1, len(blocks) - max(1, len(blocks) // 4))
    if begin > 1:
        sums = attend(blocks[1:begin], places[1:begin], sides=(1, 0), into=sums)
    rest, rest_places = blocks[begin:], places[begin:]
    crossed, rest[0] = together(crossed, rest[0])
    far_sums = attend(rest, rest_places, sides=(1,), into=[sums[0]])[0]
    far_sums, near_sums = together(far_sums, sums[1])
    near_sums = attend(rest, rest_places, sides=(0,), into=[near_sums])[0]
    far_parts = [lax.ppermute(far_sums, "seq", pairs) for pairs in far]
    near_parts = [lax.ppermute(near_sums, "seq", pairs) for pairs in near]

    mine = jnp.concatenate([mine, crossed])
    other = mine
    if split:
        mine, far_parts[-1] = together(mine, far_parts[-1])
        other = lax.ppermute(mine, "usr", [(i, i ^ 1) for i in range(usr_count)])

    blend = functools.partial(mix, seq, part, mine=mine, other=other, right=right, steps=steps)
    cut = min(len(near) + 2, count - 1)
    normed, *last = blend([near_sums] + near_parts + far_parts, picked=list(range(cut, count)))
    normed, last[0] = together(normed, last[0])
    own, *others = blend(None, picked=list(range(cut)), normed=normed)
    sends = list(zip(others + last, near + far))
    back = [lax.ppermute(o, "seq", reverse(pairs)) for o, pairs in reversed(sends)][::-1]
    return [own] + back, len(near), len(far)


def mixed_scattered(seq, queries, history_kv, lengths, token_mix):
    gathered = lax.all_gather(queries, "seq", axis=1, tiled=True)
    sums = attention(seq, lengths, [gathered], [None], history_kv, 0, gathered.shape[1], (None,))[0]
    attended = lax.psum_scatter(sums.astype(F32), "seq", scatter_dimension=1, tiled=True)
    normed = layer_norm(attended).astype(BF16)
    everyone = lax.all_gather(normed, "seq", axis=1, tiled=True)
    mixed = normed.astype(F32) + jnp.einsum("cp,upe->uce", token_mix, everyone, preferred_element_type=F32)
    return [mixed.astype(BF16)], 0, 0


def shards(seq_count, usr_count, history_kv, candidates, lengths, w_query, w_gate, token_mix, w_out, w_up, w_down):
    users, rows, width = candidates.shape
    inner = w_query.shape[1]
    seq = lax.axis_index("seq").astype(jnp.int32).reshape(1)
    flat = candidates.reshape(users * rows, width)
    queries = jnp.dot(flat, w_query, preferred_element_type=F32).astype(BF16).reshape(users, rows, inner)
    direct = seq_count & (seq_count - 1) == 0 and 2 <= seq_count <= DIRECT_MAX and users % 2 == 0
    doubled = usr_count & (usr_count - 1) == 0 and usr_count > 1
    weights = [w_up, w_down]
    if doubled:
        half = usr_count // 2
        pairs = [(i, i ^ half) for i in range(usr_count)]
        own = [[w] + narrow_exchanges(w, usr_count) for w in weights]
        came = []
    else:
        own = [[g[i] for i in range(usr_count)] for g in (lax.all_gather(w, "usr") for w in weights)]

    def held(values):
        nonlocal own, came
        values, mixing, own = together(values, token_mix, own)
        if doubled:
            came = [lax.ppermute(o[0], "usr", pairs) for o in own]
        return values, mixing

    if direct:
        pieces, nears, fars = mixed_direct(seq, queries, history_kv, lengths, token_mix, seq_count, usr_count, held)
    else:
        queries, token_mix = held(queries)
        pieces, nears, fars = mixed_scattered(seq, queries, history_kv, lengths, token_mix)
    shares = own
    if doubled:
        last = len(pieces) - 1 if fars == 0 else 1
        pieces[last], came = together(pieces[last], came)
        shares = [o + [b] + narrow_exchanges(b, usr_count) for o, b in zip(own, came)]
    return tail(seq, pieces, nears, fars, seq_count // 2 - 1, candidates, w_gate, w_out, *shares)


def solution(mesh):
    return jax.shard_map(
        functools.partial(shards, mesh.shape["seq"], mesh.shape["usr"]),
        mesh=mesh,
        in_specs=(
            P(("grp", "usr"), "seq", None),
            P(("grp", "usr"), "seq", None),
            P(("grp", "usr")),
            P(),
            P(),
            P("seq", None),
            P(),
            P(None, "usr"),
            P("usr", None),
        ),
        out_specs=P(("grp", "usr"), "seq", None),
        check_vma=False,
    )
```

```python
import functools
import math

import jax
import jax.numpy as jnp
from jax import lax
from jax.experimental import pallas as pl
from jax.experimental.pallas import tpu as pltpu
from jax.sharding import PartitionSpec as P

HEADS = 3
DH = 128
EPS = 1e-05
F32 = jnp.float32
BF16 = jnp.bfloat16
WEIGHT = 6
VMEM = pl.BlockSpec(memory_space=pltpu.VMEM)
SMEM = pl.BlockSpec(memory_space=pltpu.SMEM)


def layer_norm(values):
    center = values - jnp.mean(values, axis=-1, keepdims=True)
    spread = jnp.mean(center * center, axis=-1, keepdims=True)
    return center * lax.rsqrt(spread + EPS)


def silu(values):
    half = 0.5 * values
    return half + half * jnp.tanh(half)


def params(mib):
    return pltpu.CompilerParams(vmem_limit_bytes=mib * 1024 * 1024)


def attention_kernel(places, sides, seq_ref, lengths_ref, *refs):
    count = len(places)
    chunks, kv_ref = refs[:count], refs[count]
    outs, (q_ref, v_ref) = refs[-2 - len(sides) : -2], refs[-2:]
    _, rows, inner = chunks[0].shape
    slots = kv_ref.shape[1]
    half_scale = 0.5 / math.sqrt(DH)
    seq = seq_ref[0]
    odd = seq & 1
    total = rows * count
    block = math.gcd(total, 128)
    for out_ref, side in zip(outs, sides):
        group = out_ref.shape[0]
        first = 0 if side is None else (odd ^ side) * group
        for member in range(group):
            user = first + member
            for j, chunk in enumerate(chunks):
                q_ref[j * rows : (j + 1) * rows, :] = chunk[user]
            limit = lengths_ref[user] - seq * slots
            valid = lax.broadcasted_iota(jnp.int32, (slots, inner), 0) < limit
            v_ref[...] = jnp.where(valid, kv_ref[user, :, inner:], jnp.zeros((), BF16))
            for head in range(inner // DH):
                cols = pl.ds(head * DH, DH)
                keys = kv_ref[user, :, cols]
                values = v_ref[:, cols]
                for r in range(0, total, block):
                    scores = lax.dot_general(
                        q_ref[r : r + block, cols],
                        keys,
                        (((1,), (1,)), ((), ())),
                        preferred_element_type=F32,
                    )
                    half = scores * half_scale
                    weights = (half + half * jnp.tanh(half)).astype(BF16)
                    sums = jnp.dot(weights, values, preferred_element_type=F32).astype(BF16)
                    if places[r // rows] is None:
                        out_ref[member, r : r + block, cols] = sums
                    else:
                        start = (odd ^ places[r // rows]) * rows + r % rows
                        out_ref[member, pl.ds(pl.multiple_of(start, block), block), cols] = sums


def attention(seq, lengths, chunks, places, history_kv, total, sides, into=()):
    count = len(chunks)
    users, rows, inner = chunks[0].shape
    slots, width = history_kv.shape[1:]
    group = users if sides[0] is None else users // 2
    work = group * len(sides) * rows * count * slots * inner
    return pl.pallas_call(
        functools.partial(attention_kernel, places, sides),
        in_specs=[SMEM, SMEM] + [VMEM] * (count + 1 + len(into)),
        out_specs=[VMEM] * len(sides),
        out_shape=[jax.ShapeDtypeStruct((group, total, inner), BF16)] * len(sides),
        input_output_aliases={3 + count + i: i for i in range(len(into))},
        scratch_shapes=[pltpu.VMEM((rows * count, inner), BF16), pltpu.VMEM((slots, inner), BF16)],
        compiler_params=params(16),
        cost_estimate=pl.CostEstimate(
            flops=WEIGHT * 4 * work, bytes_accessed=2 * users * (slots * width + 2 * rows * count * inner), transcendentals=work // DH
        ),
    )(seq, lengths, *chunks, history_kv, *into)


def normed_mix(seq_ref, part_ref, mine_ref, other_ref, normed_ref, mix_ref, member, right, step, j):
    blocks, share, total = mine_ref.shape
    rows = total // blocks
    seq, part = seq_ref[0], part_ref[0]
    mix_ref[pl.ds(pl.multiple_of(part * share, share), share), :] = mine_ref[j]
    if share < rows:
        mix_ref[pl.ds(pl.multiple_of((1 - part) * share, share), share), :] = other_ref[j]
    place = jnp.clip(jnp.where(seq >= right, seq - step, seq + step), 0, blocks - 1)
    own = normed_ref[member, pl.ds(pl.multiple_of(place * rows, rows), rows), :].astype(F32)
    return (own + jnp.dot(mix_ref[...], normed_ref[member], preferred_element_type=F32)).astype(BF16)


def far_mix_kernel(sums, right, steps, picked, *refs):
    seq_ref, part_ref = refs[:2]
    parts, (mine_ref, other_ref) = refs[2 : 2 + sums], refs[2 + sums : 4 + sums]
    normed_ref, outs, mix_ref = refs[4 + sums], refs[5 + sums : -1], refs[-1]
    on_right = (seq_ref[0] >= right).astype(jnp.int32)
    rows = parts[0].shape[1]
    for member in range(normed_ref.shape[0]):
        for k in range(2):
            attended = sum(p[member].astype(F32) for p in parts[k::2])
            start = pl.multiple_of((on_right ^ k) * rows, rows)
            normed_ref[member, pl.ds(start, rows), :] = layer_norm(attended).astype(BF16)
        for out_ref, j in zip(outs, picked):
            out_ref[member] = normed_mix(
                seq_ref, part_ref, mine_ref, other_ref, normed_ref, mix_ref, member, right, steps[j], j
            )


def near_mix_kernel(right, steps, picked, *refs):
    seq_ref, part_ref, normed_ref, mine_ref, other_ref = refs[:5]
    outs, mix_ref = refs[5:-1], refs[-1]
    for member in range(normed_ref.shape[0]):
        for out_ref, j in zip(outs, picked):
            out_ref[member] = normed_mix(
                seq_ref, part_ref, mine_ref, other_ref, normed_ref, mix_ref, member, right, steps[j], j
            )


def mix(seq, part, parts, mine, other, right, steps, picked, normed=None):
    total = mine.shape[2]
    group, _, inner = (normed if parts is None else parts[0]).shape
    rows = total // len(steps)
    block = jax.ShapeDtypeStruct((group, rows, inner), BF16)
    if parts is None:
        kernel = functools.partial(near_mix_kernel, right, steps, picked)
        ops, extra = [normed], []
    else:
        kernel = functools.partial(far_mix_kernel, len(parts), right, steps, picked)
        ops, extra = parts, [jax.ShapeDtypeStruct((group, total, inner), BF16)]
    shapes = extra + [block] * len(picked)
    return pl.pallas_call(
        kernel,
        in_specs=[SMEM, SMEM] + [VMEM] * (len(ops) + 2),
        out_specs=[VMEM] * len(shapes),
        out_shape=shapes,
        scratch_shapes=[pltpu.VMEM((rows, total), BF16)],
        compiler_params=params(12),
        cost_estimate=pl.CostEstimate(
            flops=2 * group * total * inner * rows * len(picked),
            bytes_accessed=2 * total * (group * inner * (len(ops) + 1) + total),
            transcendentals=total,
        ),
    )(seq, part, *ops, mine, other)


def tail_kernel(shares, nears, fars, left, seq_ref, *refs):
    pieces, refs = refs[: 1 + nears + fars], refs[1 + nears + fars :]
    cand_ref, w_gate_ref, w_out_ref = refs[:3]
    ups, downs = refs[3 : 3 + shares], refs[3 + shares : 3 + 2 * shares]
    out_ref, mixed_ref = refs[3 + 2 * shares :]
    users, rows, width = cand_ref.shape
    inner = w_gate_ref.shape[1]
    own = pieces[0]
    if fars == 0:
        mixed_ref[...] = own[...]
    else:
        group = own.shape[0]
        seq = seq_ref[0]
        on_right = (seq > left).astype(jnp.int32)
        middle = (seq == left) | (seq == left + 1)
        for member in range(group):
            near_rows = own[member]
            if nears:
                came = functools.reduce(jnp.add, [p[member] for p in pieces[1 : 1 + nears]])
                near_rows = jnp.where(middle, near_rows, came)
            mixed_ref[on_right * group + member] = near_rows
            far_rows = functools.reduce(jnp.add, [p[member] for p in pieces[1 + nears :]])
            mixed_ref[(1 - on_right) * group + member] = far_rows
    cand = cand_ref[...].reshape(users * rows, width)
    gate = silu(jnp.dot(cand, w_gate_ref[...], preferred_element_type=F32))
    gated = (mixed_ref[...].reshape(users * rows, inner).astype(F32) * gate).astype(BF16)
    state = cand.astype(F32) + jnp.dot(gated, w_out_ref[...], preferred_element_type=F32)
    ffn_in = layer_norm(state).astype(BF16)
    total = state
    for up, down in zip(ups, downs):
        hidden = jax.nn.gelu(jnp.dot(ffn_in, up[...], preferred_element_type=F32)).astype(BF16)
        total = total + jnp.dot(hidden, down[...], preferred_element_type=F32)
    out_ref[...] = total.astype(BF16).reshape(users, rows, width)


def tail(seq, pieces, nears, fars, left, candidates, w_gate, w_out, ups, downs):
    users, rows, width = candidates.shape
    inner = w_gate.shape[1]
    hidden = sum(up.shape[1] for up in ups)
    total = users * rows
    return pl.pallas_call(
        functools.partial(tail_kernel, len(ups), nears, fars, left),
        in_specs=[SMEM] + [VMEM] * (len(pieces) + 3 + 2 * len(ups)),
        out_specs=VMEM,
        out_shape=jax.ShapeDtypeStruct((users, rows, width), BF16),
        scratch_shapes=[pltpu.VMEM((users, rows, inner), BF16)],
        compiler_params=params(24),
        cost_estimate=pl.CostEstimate(
            flops=2 * total * width * (2 * inner + 2 * hidden),
            bytes_accessed=2 * width * (2 * hidden + inner + 2 * total),
            transcendentals=total * hidden,
        ),
    )(seq, *pieces, candidates, w_gate, w_out, *ups, *downs)


def narrow_exchanges(share, count):
    held = [share]
    step = count // 4
    while step:
        held = held + [lax.ppermute(a, "usr", [(i, i ^ step) for i in range(count)]) for a in held]
        step //= 2
    return held[1:]


def middle_pairs(count):
    left, right = count // 2 - 1, count // 2
    near = [[(left - d, left), (right + d, right)] for d in range(1, count // 2)]
    far = [[(left - d, right), (right + d, left)] for d in range(count // 2)]
    return near, far


def reverse(pairs):
    return [(b, a) for a, b in pairs]


def together(*values):
    return lax.optimization_barrier(values)


def mixed_by_pairs(seq, queries, history_kv, lengths, token_mix, usr_count, own, first_wide, second_wide):
    count, right = 4, 2
    near, far = middle_pairs(count)
    mate, cross = [[(i, i ^ k) for i in range(count)] for k in (1, 2)]
    rows = queries.shape[1]
    total = rows * count
    place = lax.axis_index("usr").astype(jnp.int32)
    attend = functools.partial(attention, seq, lengths, history_kv=history_kv, total=2 * rows)

    crossed = lax.ppermute(queries, "seq", cross)
    mated = lax.ppermute(queries, "seq", mate)
    give_own, keep_own = attend([queries], [0], sides=(0, 1))

    token_mix, own = together(token_mix, own)
    split = usr_count % 2 == 0 and rows % 32 == 0
    part = (place % 2 if split else jnp.zeros((), jnp.int32)).reshape(1)
    piece = token_mix
    if split:
        piece = lax.dynamic_slice_in_dim(piece, part[0] * (rows // 2), rows // 2, 0)
    mine = jnp.stack([piece] + [lax.ppermute(piece, "seq", pairs) for pairs in near])
    steps = [0] + [-d for d in range(1, count // 2)] + [d + 1 for d in range(count // 2)]

    give_own, keep_own = attend([mated], [1], sides=(0, 1), into=[give_own, keep_own])
    mine, crossed, give_own, keep_own = together(mine, crossed, give_own, keep_own)
    opposite = lax.ppermute(crossed, "seq", mate)
    given_own = lax.ppermute(give_own, "seq", mate)
    swapped = lax.ppermute(mine, "seq", far[0])
    give_other, keep_other = attend([crossed], [0], sides=(0, 1))
    swapped, opposite, first_wide = together(swapped, opposite, first_wide)
    second_wide = second_wide()
    give_other = attend([opposite], [1], sides=(0,), into=[give_other])[0]
    give_other, keep_other = together(give_other, keep_other)
    given_other = lax.ppermute(give_other, "seq", mate)
    keep_other = attend([opposite], [1], sides=(1,), into=[keep_other])[0]

    ends = far[-1]
    keep_own = keep_own + given_own
    came_other = lax.ppermute(keep_own, "seq", ends)
    keep_other = keep_other + given_other
    came_own = lax.ppermute(keep_other, "seq", ends)

    mine = jnp.concatenate([mine, swapped])
    other = mine
    if split:
        other = lax.ppermute(mine, "usr", [(i, i ^ 1) for i in range(usr_count)])

    blend = functools.partial(mix, seq, part, mine=mine, other=other, right=right, steps=steps)
    cut = count - 1
    normed, *last = blend([keep_own, keep_other, came_own, came_other], picked=list(range(cut, count)))
    normed, last[0] = together(normed, last[0])
    mixed, *others = blend(None, picked=list(range(cut)), normed=normed)
    sends = list(zip(others + last, near + far))
    back = [lax.ppermute(o, "seq", reverse(pairs)) for o, pairs in reversed(sends)][::-1]
    return [mixed] + back, len(near), len(far), own, [first_wide, second_wide]


def mixed_scattered(seq, queries, history_kv, lengths, token_mix):
    gathered = lax.all_gather(queries, "seq", axis=1, tiled=True)
    sums = attention(seq, lengths, [gathered], [None], history_kv, gathered.shape[1], (None,))[0]
    attended = lax.psum_scatter(sums.astype(F32), "seq", scatter_dimension=1, tiled=True)
    normed = layer_norm(attended).astype(BF16)
    everyone = lax.all_gather(normed, "seq", axis=1, tiled=True)
    mixed = normed.astype(F32) + jnp.einsum("cp,upe->uce", token_mix, everyone, preferred_element_type=F32)
    return [mixed.astype(BF16)], 0, 0


def shards(seq_count, usr_count, history_kv, candidates, lengths, w_query, w_gate, token_mix, w_out, w_up, w_down):
    users, rows, width = candidates.shape
    inner = w_query.shape[1]
    seq = lax.axis_index("seq").astype(jnp.int32).reshape(1)
    flat = candidates.reshape(users * rows, width)
    queries = jnp.dot(flat, w_query, preferred_element_type=F32).astype(BF16).reshape(users, rows, inner)
    by_pairs = seq_count == 4 and users % 2 == 0
    doubled = usr_count & (usr_count - 1) == 0 and usr_count > 1
    weights = [w_up, w_down]
    half = usr_count // 2
    widest = [(i, i ^ half) for i in range(usr_count)]
    if doubled:
        own = [[w] + narrow_exchanges(w, usr_count) for w in weights]
        wide = lax.ppermute(w_up, "usr", widest)
    else:
        own = [[g[i] for i in range(usr_count)] for g in (lax.all_gather(w, "usr") for w in weights)]
        wide = w_up

    def second():
        return lax.ppermute(w_down, "usr", widest) if doubled else w_down

    if by_pairs:
        pieces, nears, fars, own, wide = mixed_by_pairs(
            seq, queries, history_kv, lengths, token_mix, usr_count, own, wide, second
        )
    else:
        pieces, nears, fars = mixed_scattered(seq, queries, history_kv, lengths, token_mix)
        wide = [wide, second()]
    shares = own
    if doubled:
        pieces[0], wide = together(pieces[0], wide)
        shares = [o + [b] + narrow_exchanges(b, usr_count) for o, b in zip(own, wide)]
    return tail(seq, pieces, nears, fars, seq_count // 2 - 1, candidates, w_gate, w_out, *shares)


def solution(mesh):
    return jax.shard_map(
        functools.partial(shards, mesh.shape["seq"], mesh.shape["usr"]),
        mesh=mesh,
        in_specs=(
            P(("grp", "usr"), "seq", None),
            P(("grp", "usr"), "seq", None),
            P(("grp", "usr")),
            P(),
            P(),
            P("seq", None),
            P(),
            P(None, "usr"),
            P("usr", None),
        ),
        out_specs=P(("grp", "usr"), "seq", None),
        check_vma=False,
    )
```

```python
import functools
import math

import jax
import jax.numpy as jnp
from jax import lax
from jax.experimental import pallas as pl
from jax.experimental.pallas import tpu as pltpu
from jax.sharding import PartitionSpec as P

HEADS = 3
DH = 128
EPS = 1e-05
F32 = jnp.float32
BF16 = jnp.bfloat16
WEIGHT = 3
VMEM = pl.BlockSpec(memory_space=pltpu.VMEM)
SMEM = pl.BlockSpec(memory_space=pltpu.SMEM)


def layer_norm(values):
    center = values - jnp.mean(values, axis=-1, keepdims=True)
    spread = jnp.mean(center * center, axis=-1, keepdims=True)
    return center * lax.rsqrt(spread + EPS)


def silu(values):
    half = 0.5 * values
    return half + half * jnp.tanh(half)


def params(mib):
    return pltpu.CompilerParams(vmem_limit_bytes=mib * 1024 * 1024)


def attention_kernel(places, sides, seq_ref, lengths_ref, *refs):
    count = len(places)
    chunks, kv_ref = refs[:count], refs[count]
    outs, (q_ref, v_ref) = refs[-2 - len(sides) : -2], refs[-2:]
    _, rows, inner = chunks[0].shape
    slots = kv_ref.shape[1]
    half_scale = 0.5 / math.sqrt(DH)
    seq = seq_ref[0]
    odd = seq & 1
    total = rows * count
    block = math.gcd(total, 128)
    for out_ref, side in zip(outs, sides):
        group = out_ref.shape[0]
        first = 0 if side is None else (odd ^ side) * group
        for member in range(group):
            user = first + member
            for j, chunk in enumerate(chunks):
                q_ref[j * rows : (j + 1) * rows, :] = chunk[user]
            limit = lengths_ref[user] - seq * slots
            valid = lax.broadcasted_iota(jnp.int32, (slots, inner), 0) < limit
            v_ref[...] = jnp.where(valid, kv_ref[user, :, inner:], jnp.zeros((), BF16))
            for head in range(inner // DH):
                cols = pl.ds(head * DH, DH)
                keys = kv_ref[user, :, cols]
                values = v_ref[:, cols]
                for r in range(0, total, block):
                    scores = lax.dot_general(
                        q_ref[r : r + block, cols],
                        keys,
                        (((1,), (1,)), ((), ())),
                        preferred_element_type=F32,
                    )
                    half = scores * half_scale
                    weights = (half + half * jnp.tanh(half)).astype(BF16)
                    sums = jnp.dot(weights, values, preferred_element_type=F32).astype(BF16)
                    if places[r // rows] is None:
                        out_ref[member, r : r + block, cols] = sums
                    else:
                        start = (odd ^ places[r // rows]) * rows + r % rows
                        out_ref[member, pl.ds(pl.multiple_of(start, block), block), cols] = sums


def attention(seq, lengths, chunks, places, history_kv, total, sides, into=()):
    count = len(chunks)
    users, rows, inner = chunks[0].shape
    slots, width = history_kv.shape[1:]
    group = users if sides[0] is None else users // 2
    work = group * len(sides) * rows * count * slots * inner
    return pl.pallas_call(
        functools.partial(attention_kernel, places, sides),
        in_specs=[SMEM, SMEM] + [VMEM] * (count + 1 + len(into)),
        out_specs=[VMEM] * len(sides),
        out_shape=[jax.ShapeDtypeStruct((group, total, inner), BF16)] * len(sides),
        input_output_aliases={3 + count + i: i for i in range(len(into))},
        scratch_shapes=[pltpu.VMEM((rows * count, inner), BF16), pltpu.VMEM((slots, inner), BF16)],
        compiler_params=params(16),
        cost_estimate=pl.CostEstimate(
            flops=WEIGHT * 4 * work, bytes_accessed=2 * users * (slots * width + 2 * rows * count * inner), transcendentals=work // DH
        ),
    )(seq, lengths, *chunks, history_kv, *into)


def mix_kernel(seq_ref, *refs):
    parts, (own_mix_ref, mate_mix_ref, own_ref, mate_ref, normed_ref) = refs[:-5], refs[-5:]
    seq = seq_ref[0]
    pair = seq >> 1
    half = parts[0].shape[1]
    rows = half // 2
    for member in range(parts[0].shape[0]):
        for k in range(2):
            attended = sum(p[member].astype(F32) for p in parts[k::2])
            start = pl.multiple_of((pair ^ k) * half, half)
            normed_ref[pl.ds(start, half), :] = layer_norm(attended).astype(BF16)
        for place, mix_ref, out_ref in ((seq ^ 1, mate_mix_ref, mate_ref), (seq, own_mix_ref, own_ref)):
            own = normed_ref[pl.ds(pl.multiple_of(place * rows, rows), rows), :].astype(F32)
            mixed = own + jnp.dot(mix_ref[...], normed_ref[...], preferred_element_type=F32)
            out_ref[member] = mixed.astype(BF16)


def mix(seq, parts, own_mix, mate_mix):
    group, _, inner = parts[0].shape
    rows, total = own_mix.shape
    return pl.pallas_call(
        mix_kernel,
        in_specs=[SMEM] + [VMEM] * (len(parts) + 2),
        out_specs=[VMEM] * 2,
        out_shape=[jax.ShapeDtypeStruct((group, rows, inner), BF16)] * 2,
        scratch_shapes=[pltpu.VMEM((total, inner), BF16)],
        compiler_params=params(12),
        cost_estimate=pl.CostEstimate(
            flops=4 * group * total * inner * rows,
            bytes_accessed=2 * total * (group * inner * len(parts) + 2 * rows),
            transcendentals=total,
        ),
    )(seq, *parts, own_mix, mate_mix)


def tail_kernel(shares, count, seq_ref, *refs):
    pieces, refs = refs[:count], refs[count:]
    cand_ref, w_gate_ref, w_out_ref = refs[:3]
    ups, downs = refs[3 : 3 + shares], refs[3 + shares : 3 + 2 * shares]
    out_ref, mixed_ref = refs[3 + 2 * shares :]
    users, rows, width = cand_ref.shape
    inner = w_gate_ref.shape[1]
    if count == 1:
        mixed_ref[...] = pieces[0][...]
    else:
        group = pieces[0].shape[0]
        odd = seq_ref[0] & 1
        for k, piece in enumerate(pieces):
            for member in range(group):
                mixed_ref[(odd ^ 1 ^ k) * group + member] = piece[member]
    cand = cand_ref[...].reshape(users * rows, width)
    gate = silu(jnp.dot(cand, w_gate_ref[...], preferred_element_type=F32))
    gated = (mixed_ref[...].reshape(users * rows, inner).astype(F32) * gate).astype(BF16)
    state = cand.astype(F32) + jnp.dot(gated, w_out_ref[...], preferred_element_type=F32)
    ffn_in = layer_norm(state).astype(BF16)
    total = state
    for up, down in zip(ups, downs):
        hidden = jax.nn.gelu(jnp.dot(ffn_in, up[...], preferred_element_type=F32)).astype(BF16)
        total = total + jnp.dot(hidden, down[...], preferred_element_type=F32)
    out_ref[...] = total.astype(BF16).reshape(users, rows, width)


def tail(seq, pieces, candidates, w_gate, w_out, ups, downs):
    users, rows, width = candidates.shape
    inner = w_gate.shape[1]
    hidden = sum(up.shape[1] for up in ups)
    total = users * rows
    return pl.pallas_call(
        functools.partial(tail_kernel, len(ups), len(pieces)),
        in_specs=[SMEM] + [VMEM] * (len(pieces) + 3 + 2 * len(ups)),
        out_specs=VMEM,
        out_shape=jax.ShapeDtypeStruct((users, rows, width), BF16),
        scratch_shapes=[pltpu.VMEM((users, rows, inner), BF16)],
        compiler_params=params(24),
        cost_estimate=pl.CostEstimate(
            flops=2 * total * width * (2 * inner + 2 * hidden),
            bytes_accessed=2 * width * (2 * hidden + inner + 2 * total),
            transcendentals=total * hidden,
        ),
    )(seq, *pieces, candidates, w_gate, w_out, *ups, *downs)


def narrow_exchanges(share, count):
    held = [share]
    step = count // 4
    while step:
        held = held + [lax.ppermute(a, "usr", [(i, i ^ step) for i in range(count)]) for a in held]
        step //= 2
    return held[1:]


def together(*values):
    return lax.optimization_barrier(values)


def mixed_by_pairs(seq, queries, history_kv, lengths, token_mix, own, first_wide, second_wide):
    count = 4
    mate, cross = [[(i, i ^ k) for i in range(count)] for k in (1, 2)]
    attend = functools.partial(attention, seq, lengths, history_kv=history_kv, total=2 * queries.shape[1])

    crossed = lax.ppermute(queries, "seq", cross)
    mated = lax.ppermute(queries, "seq", mate)
    give_own, keep_own = attend([queries], [0], sides=(0, 1))
    give_own, keep_own = attend([mated], [1], sides=(0, 1), into=[give_own, keep_own])
    crossed, give_own, keep_own, own, token_mix = together(crossed, give_own, keep_own, own, token_mix)
    opposite = lax.ppermute(crossed, "seq", mate)
    given_own = lax.ppermute(give_own, "seq", mate)
    give_other, keep_other = attend([crossed], [0], sides=(0, 1))
    opposite, first_wide = together(opposite, first_wide)
    second_wide = second_wide(own)
    give_other = attend([opposite], [1], sides=(0,), into=[give_other])[0]
    give_other, keep_other = together(give_other, keep_other)
    given_other = lax.ppermute(give_other, "seq", mate)
    keep_other = attend([opposite], [1], sides=(1,), into=[keep_other])[0]

    keep_own = keep_own + given_own
    came_other = lax.ppermute(keep_own, "seq", cross)
    keep_other = keep_other + given_other
    came_own = lax.ppermute(keep_other, "seq", cross)

    mate_mix = lax.ppermute(token_mix, "seq", mate)
    mixed, mate_mixed = mix(seq, [keep_own, keep_other, came_own, came_other], token_mix, mate_mix)
    return [mixed, lax.ppermute(mate_mixed, "seq", mate)], own, [first_wide, second_wide]


def mixed_scattered(seq, queries, history_kv, lengths, token_mix):
    gathered = lax.all_gather(queries, "seq", axis=1, tiled=True)
    sums = attention(seq, lengths, [gathered], [None], history_kv, gathered.shape[1], (None,))[0]
    attended = lax.psum_scatter(sums.astype(F32), "seq", scatter_dimension=1, tiled=True)
    normed = layer_norm(attended).astype(BF16)
    everyone = lax.all_gather(normed, "seq", axis=1, tiled=True)
    mixed = normed.astype(F32) + jnp.einsum("cp,upe->uce", token_mix, everyone, preferred_element_type=F32)
    return [mixed.astype(BF16)]


def shards(seq_count, usr_count, history_kv, candidates, lengths, w_query, w_gate, token_mix, w_out, w_up, w_down):
    users, rows, width = candidates.shape
    inner = w_query.shape[1]
    seq = lax.axis_index("seq").astype(jnp.int32).reshape(1)
    flat = candidates.reshape(users * rows, width)
    queries = jnp.dot(flat, w_query, preferred_element_type=F32).astype(BF16).reshape(users, rows, inner)
    by_pairs = seq_count == 4 and users % 2 == 0
    doubled = usr_count & (usr_count - 1) == 0 and usr_count > 1
    weights = [w_up, w_down]
    half = usr_count // 2
    widest = [(i, i ^ half) for i in range(usr_count)]
    if doubled:
        own = [[w] + narrow_exchanges(w, usr_count) for w in weights]
        wide = lax.ppermute(w_up, "usr", widest)
    else:
        own = [[g[i] for i in range(usr_count)] for g in (lax.all_gather(w, "usr") for w in weights)]
        wide = w_up

    def second(own):
        return lax.ppermute(own[1][0], "usr", widest) if doubled else w_down

    if by_pairs:
        pieces, own, wide = mixed_by_pairs(seq, queries, history_kv, lengths, token_mix, own, wide, second)
    else:
        pieces = mixed_scattered(seq, queries, history_kv, lengths, token_mix)
        wide = [wide, second(own)]
    shares = own
    if doubled:
        pieces[0], wide = together(pieces[0], wide)
        shares = [o + [b] + narrow_exchanges(b, usr_count) for o, b in zip(own, wide)]
    return tail(seq, pieces, candidates, w_gate, w_out, *shares)


def solution(mesh):
    return jax.shard_map(
        functools.partial(shards, mesh.shape["seq"], mesh.shape["usr"]),
        mesh=mesh,
        in_specs=(
            P(("grp", "usr"), "seq", None),
            P(("grp", "usr"), "seq", None),
            P(("grp", "usr")),
            P(),
            P(),
            P("seq", None),
            P(),
            P(None, "usr"),
            P("usr", None),
        ),
        out_specs=P(("grp", "usr"), "seq", None),
        check_vma=False,
    )
```

```python
import functools
import math

import jax
import jax.numpy as jnp
from jax import lax
from jax.experimental import pallas as pl
from jax.experimental.pallas import tpu as pltpu
from jax.sharding import PartitionSpec as P

HEADS = 3
DH = 128
EPS = 1e-05
F32 = jnp.float32
BF16 = jnp.bfloat16
WEIGHT = 3
VMEM = pl.BlockSpec(memory_space=pltpu.VMEM)
SMEM = pl.BlockSpec(memory_space=pltpu.SMEM)


def layer_norm(values):
    center = values - jnp.mean(values, axis=-1, keepdims=True)
    spread = jnp.mean(center * center, axis=-1, keepdims=True)
    return center * lax.rsqrt(spread + EPS)


def silu(values):
    half = 0.5 * values
    return half + half * jnp.tanh(half)


def params(mib):
    return pltpu.CompilerParams(vmem_limit_bytes=mib * 1024 * 1024)


def attention_kernel(places, sides, seq_ref, lengths_ref, *refs):
    count = len(places)
    chunks, kv_ref = refs[:count], refs[count]
    outs, (q_ref, v_ref) = refs[-2 - len(sides) : -2], refs[-2:]
    _, rows, inner = chunks[0].shape
    slots = kv_ref.shape[1]
    half_scale = 0.5 / math.sqrt(DH)
    seq = seq_ref[0]
    odd = seq & 1
    total = rows * count
    block = math.gcd(total, 128)
    for out_ref, side in zip(outs, sides):
        group = out_ref.shape[0]
        first = 0 if side is None else (odd ^ side) * group
        for member in range(group):
            user = first + member
            for j, chunk in enumerate(chunks):
                q_ref[j * rows : (j + 1) * rows, :] = chunk[user]
            limit = lengths_ref[user] - seq * slots
            valid = lax.broadcasted_iota(jnp.int32, (slots, inner), 0) < limit
            v_ref[...] = jnp.where(valid, kv_ref[user, :, inner:], jnp.zeros((), BF16))
            for head in range(inner // DH):
                cols = pl.ds(head * DH, DH)
                keys = kv_ref[user, :, cols]
                values = v_ref[:, cols]
                for r in range(0, total, block):
                    scores = lax.dot_general(
                        q_ref[r : r + block, cols],
                        keys,
                        (((1,), (1,)), ((), ())),
                        preferred_element_type=F32,
                    )
                    half = scores * half_scale
                    weights = (half + half * jnp.tanh(half)).astype(BF16)
                    sums = jnp.dot(weights, values, preferred_element_type=F32).astype(BF16)
                    if places[r // rows] is None:
                        out_ref[member, r : r + block, cols] = sums
                    else:
                        start = (odd ^ places[r // rows]) * rows + r % rows
                        out_ref[member, pl.ds(pl.multiple_of(start, block), block), cols] = sums


def attention(seq, lengths, chunks, places, history_kv, total, sides, into=()):
    count = len(chunks)
    users, rows, inner = chunks[0].shape
    slots, width = history_kv.shape[1:]
    group = users if sides[0] is None else users // 2
    work = group * len(sides) * rows * count * slots * inner
    return pl.pallas_call(
        functools.partial(attention_kernel, places, sides),
        in_specs=[SMEM, SMEM] + [VMEM] * (count + 1 + len(into)),
        out_specs=[VMEM] * len(sides),
        out_shape=[jax.ShapeDtypeStruct((group, total, inner), BF16)] * len(sides),
        input_output_aliases={3 + count + i: i for i in range(len(into))},
        scratch_shapes=[pltpu.VMEM((rows * count, inner), BF16), pltpu.VMEM((slots, inner), BF16)],
        compiler_params=params(16),
        cost_estimate=pl.CostEstimate(
            flops=WEIGHT * 4 * work, bytes_accessed=2 * users * (slots * width + 2 * rows * count * inner), transcendentals=work // DH
        ),
    )(seq, lengths, *chunks, history_kv, *into)


def mix_kernel(seq_ref, *refs):
    parts, (own_mix_ref, mate_mix_ref, own_ref, mate_ref, normed_ref) = refs[:-5], refs[-5:]
    seq = seq_ref[0]
    pair = seq >> 1
    half = parts[0].shape[1]
    rows = half // 2
    for member in range(parts[0].shape[0]):
        for k in range(2):
            attended = sum(p[member].astype(F32) for p in parts[k::2])
            start = pl.multiple_of((pair ^ k) * half, half)
            normed_ref[pl.ds(start, half), :] = layer_norm(attended).astype(BF16)
        for place, mix_ref, out_ref in ((seq ^ 1, mate_mix_ref, mate_ref), (seq, own_mix_ref, own_ref)):
            own = normed_ref[pl.ds(pl.multiple_of(place * rows, rows), rows), :].astype(F32)
            mixed = own + jnp.dot(mix_ref[...], normed_ref[...], preferred_element_type=F32)
            out_ref[member] = mixed.astype(BF16)


def mix(seq, parts, own_mix, mate_mix):
    group, _, inner = parts[0].shape
    rows, total = own_mix.shape
    return pl.pallas_call(
        mix_kernel,
        in_specs=[SMEM] + [VMEM] * (len(parts) + 2),
        out_specs=[VMEM] * 2,
        out_shape=[jax.ShapeDtypeStruct((group, rows, inner), BF16)] * 2,
        scratch_shapes=[pltpu.VMEM((total, inner), BF16)],
        compiler_params=params(12),
        cost_estimate=pl.CostEstimate(
            flops=4 * group * total * inner * rows,
            bytes_accessed=2 * total * (group * inner * len(parts) + 2 * rows),
            transcendentals=total,
        ),
    )(seq, *parts, own_mix, mate_mix)


def tail_kernel(shares, count, seq_ref, *refs):
    pieces, refs = refs[:count], refs[count:]
    cand_ref, w_gate_ref, w_out_ref = refs[:3]
    ups, downs = refs[3 : 3 + shares], refs[3 + shares : 3 + 2 * shares]
    out_ref, mixed_ref = refs[3 + 2 * shares :]
    users, rows, width = cand_ref.shape
    inner = w_gate_ref.shape[1]
    if count == 1:
        mixed_ref[...] = pieces[0][...]
    else:
        group = pieces[0].shape[0]
        odd = seq_ref[0] & 1
        for k, piece in enumerate(pieces):
            for member in range(group):
                mixed_ref[(odd ^ 1 ^ k) * group + member] = piece[member]
    cand = cand_ref[...].reshape(users * rows, width)
    gate = silu(jnp.dot(cand, w_gate_ref[...], preferred_element_type=F32))
    gated = (mixed_ref[...].reshape(users * rows, inner).astype(F32) * gate).astype(BF16)
    state = cand.astype(F32) + jnp.dot(gated, w_out_ref[...], preferred_element_type=F32)
    ffn_in = layer_norm(state).astype(BF16)
    total = state
    for up, down in zip(ups, downs):
        hidden = jax.nn.gelu(jnp.dot(ffn_in, up[...], preferred_element_type=F32)).astype(BF16)
        total = total + jnp.dot(hidden, down[...], preferred_element_type=F32)
    out_ref[...] = total.astype(BF16).reshape(users, rows, width)


def tail(seq, pieces, candidates, w_gate, w_out, ups, downs):
    users, rows, width = candidates.shape
    inner = w_gate.shape[1]
    hidden = sum(up.shape[1] for up in ups)
    total = users * rows
    return pl.pallas_call(
        functools.partial(tail_kernel, len(ups), len(pieces)),
        in_specs=[SMEM] + [VMEM] * (len(pieces) + 3 + 2 * len(ups)),
        out_specs=VMEM,
        out_shape=jax.ShapeDtypeStruct((users, rows, width), BF16),
        scratch_shapes=[pltpu.VMEM((users, rows, inner), BF16)],
        compiler_params=params(24),
        cost_estimate=pl.CostEstimate(
            flops=2 * total * width * (2 * inner + 2 * hidden),
            bytes_accessed=2 * width * (2 * hidden + inner + 2 * total),
            transcendentals=total * hidden,
        ),
    )(seq, *pieces, candidates, w_gate, w_out, *ups, *downs)


def narrow_exchanges(share, count):
    held = [share]
    step = count // 4
    while step:
        held = held + [lax.ppermute(a, "usr", [(i, i ^ step) for i in range(count)]) for a in held]
        step //= 2
    return held[1:]


def together(*values):
    return lax.optimization_barrier(values)


def mixed_by_pairs(seq, queries, later, history_kv, lengths, token_mix, own, first_wide, second_wide):
    count = 4
    mate, cross = [[(i, i ^ k) for i in range(count)] for k in (1, 2)]
    attend = functools.partial(attention, seq, lengths, history_kv=history_kv, total=2 * queries.shape[1])

    crossed = lax.ppermute(queries, "seq", cross)
    mated = lax.ppermute(queries, "seq", mate)
    give_own, keep_own = attend([later], [0], sides=(0, 1))
    give_own, keep_own = attend([mated], [1], sides=(0, 1), into=[give_own, keep_own])
    crossed, give_own, keep_own, own, token_mix = together(crossed, give_own, keep_own, own, token_mix)
    opposite = lax.ppermute(crossed, "seq", mate)
    given_own = lax.ppermute(give_own, "seq", mate)
    give_other, keep_other = attend([crossed], [0], sides=(0, 1))
    opposite, first_wide = together(opposite, first_wide)
    second_wide = second_wide(own)
    give_other = attend([opposite], [1], sides=(0,), into=[give_other])[0]
    give_other, keep_other = together(give_other, keep_other)
    given_other = lax.ppermute(give_other, "seq", mate)
    keep_other = attend([opposite], [1], sides=(1,), into=[keep_other])[0]

    keep_own = keep_own + given_own
    came_other = lax.ppermute(keep_own, "seq", cross)
    keep_other = keep_other + given_other
    came_own = lax.ppermute(keep_other, "seq", cross)

    mate_mix = lax.ppermute(token_mix, "seq", mate)
    mixed, mate_mixed = mix(seq, [keep_own, keep_other, came_own, came_other], token_mix, mate_mix)
    return [mixed, lax.ppermute(mate_mixed, "seq", mate)], own, [first_wide, second_wide]


def mixed_scattered(seq, queries, history_kv, lengths, token_mix):
    gathered = lax.all_gather(queries, "seq", axis=1, tiled=True)
    sums = attention(seq, lengths, [gathered], [None], history_kv, gathered.shape[1], (None,))[0]
    attended = lax.psum_scatter(sums.astype(F32), "seq", scatter_dimension=1, tiled=True)
    normed = layer_norm(attended).astype(BF16)
    everyone = lax.all_gather(normed, "seq", axis=1, tiled=True)
    mixed = normed.astype(F32) + jnp.einsum("cp,upe->uce", token_mix, everyone, preferred_element_type=F32)
    return [mixed.astype(BF16)]


def shards(seq_count, usr_count, history_kv, candidates, lengths, w_query, w_gate, token_mix, w_out, w_up, w_down):
    users, rows, width = candidates.shape
    inner = w_query.shape[1]
    seq = lax.axis_index("seq").astype(jnp.int32).reshape(1)
    flat = candidates.reshape(users * rows, width)
    queries = jnp.dot(flat, w_query, preferred_element_type=F32).astype(BF16).reshape(users, rows, inner)
    by_pairs = seq_count == 4 and users % 2 == 0
    doubled = usr_count & (usr_count - 1) == 0 and usr_count > 1
    later, weights = together(queries, [w_up, w_down])
    half = usr_count // 2
    widest = [(i, i ^ half) for i in range(usr_count)]
    if doubled:
        own = [[w] + narrow_exchanges(v, usr_count) for v, w in zip((w_up, w_down), weights)]
        wide = lax.ppermute(weights[0], "usr", widest)
    else:
        own = [[g[i] for i in range(usr_count)] for g in (lax.all_gather(w, "usr") for w in weights)]
        wide = w_up

    def second(own):
        return lax.ppermute(own[1][0], "usr", widest) if doubled else w_down

    if by_pairs:
        pieces, own, wide = mixed_by_pairs(seq, queries, later, history_kv, lengths, token_mix, own, wide, second)
    else:
        pieces = mixed_scattered(seq, later, history_kv, lengths, token_mix)
        wide = [wide, second(own)]
    shares = own
    if doubled:
        pieces[0], wide = together(pieces[0], wide)
        shares = [o + [b] + narrow_exchanges(b, usr_count) for o, b in zip(own, wide)]
    return tail(seq, pieces, candidates, w_gate, w_out, *shares)


def solution(mesh):
    return jax.shard_map(
        functools.partial(shards, mesh.shape["seq"], mesh.shape["usr"]),
        mesh=mesh,
        in_specs=(
            P(("grp", "usr"), "seq", None),
            P(("grp", "usr"), "seq", None),
            P(("grp", "usr")),
            P(),
            P(),
            P("seq", None),
            P(),
            P(None, "usr"),
            P("usr", None),
        ),
        out_specs=P(("grp", "usr"), "seq", None),
        check_vma=False,
    )
```

```python
import functools
import math

import jax
import jax.numpy as jnp
from jax import lax
from jax.experimental import pallas as pl
from jax.experimental.pallas import tpu as pltpu
from jax.sharding import PartitionSpec as P

HEADS = 3
DH = 128
EPS = 1e-05
F32 = jnp.float32
BF16 = jnp.bfloat16
WEIGHT = 3
VMEM = pl.BlockSpec(memory_space=pltpu.VMEM)
SMEM = pl.BlockSpec(memory_space=pltpu.SMEM)


def layer_norm(values):
    center = values - jnp.mean(values, axis=-1, keepdims=True)
    spread = jnp.mean(center * center, axis=-1, keepdims=True)
    return center * lax.rsqrt(spread + EPS)


def silu(values):
    half = 0.5 * values
    return half + half * jnp.tanh(half)


def gelu(values):
    scale = math.sqrt(2 / math.pi)
    half = 0.5 * values
    return half + half * jnp.tanh(values * (scale + (scale * 0.044715) * (values * values)))


def params(mib):
    return pltpu.CompilerParams(vmem_limit_bytes=mib * 1024 * 1024)


def attention_kernel(places, sides, seq_ref, lengths_ref, *refs):
    count = len(places)
    chunks, kv_ref = refs[:count], refs[count]
    outs = refs[-len(sides) :]
    _, rows, inner = chunks[0].shape
    slots = kv_ref.shape[1]
    half_scale = 0.5 / math.sqrt(DH)
    seq = seq_ref[0]
    odd = seq & 1
    block = math.gcd(rows, 128)
    for out_ref, side in zip(outs, sides):
        group = out_ref.shape[0]
        first = 0 if side is None else (odd ^ side) * group
        for member in range(group):
            user = first + member
            limit = lengths_ref[user] - seq * slots
            valid = lax.broadcasted_iota(jnp.int32, (slots, DH), 0) < limit
            heads = [slice(h * DH, (h + 1) * DH) for h in range(inner // DH)]
            values = [
                jnp.where(valid, kv_ref[user, :, inner + c.start : inner + c.stop], jnp.zeros((), BF16)) for c in heads
            ]
            for j, chunk in enumerate(chunks):
                for r in range(0, rows, block):
                    halves = [
                        half_scale
                        * lax.dot_general(
                            chunk[user, r : r + block, c],
                            kv_ref[user, :, c],
                            (((1,), (1,)), ((), ())),
                            preferred_element_type=F32,
                        )
                        for c in heads
                    ]
                    weights = [(half + half * jnp.tanh(half)).astype(BF16) for half in halves]
                    sums = [jnp.dot(w, v, preferred_element_type=F32).astype(BF16) for w, v in zip(weights, values)]
                    start = r if places[j] is None else pl.multiple_of((odd ^ places[j]) * rows + r, block)
                    out_ref[member, pl.ds(start, block), :] = jnp.concatenate(sums, axis=1)


def attention(seq, lengths, chunks, places, history_kv, total, sides, into=()):
    count = len(chunks)
    users, rows, inner = chunks[0].shape
    slots, width = history_kv.shape[1:]
    group = users if sides[0] is None else users // 2
    work = group * len(sides) * rows * count * slots * inner
    return pl.pallas_call(
        functools.partial(attention_kernel, places, sides),
        in_specs=[SMEM, SMEM] + [VMEM] * (count + 1 + len(into)),
        out_specs=[VMEM] * len(sides),
        out_shape=[jax.ShapeDtypeStruct((group, total, inner), BF16)] * len(sides),
        input_output_aliases={3 + count + i: i for i in range(len(into))},
        compiler_params=params(16),
        cost_estimate=pl.CostEstimate(
            flops=WEIGHT * 4 * work, bytes_accessed=2 * users * (slots * width + 2 * rows * count * inner), transcendentals=work // DH
        ),
    )(seq, lengths, *chunks, history_kv, *into)


def mix_kernel(seq_ref, *refs):
    parts, (own_mix_ref, mate_mix_ref, own_ref, mate_ref, normed_ref) = refs[:-5], refs[-5:]
    seq = seq_ref[0]
    pair = seq >> 1
    half = parts[0].shape[1]
    rows = half // 2
    for member in range(parts[0].shape[0]):
        for k in range(2):
            attended = sum(p[member].astype(F32) for p in parts[k::2])
            start = pl.multiple_of((pair ^ k) * half, half)
            normed_ref[pl.ds(start, half), :] = layer_norm(attended).astype(BF16)
        for place, mix_ref, out_ref in ((seq ^ 1, mate_mix_ref, mate_ref), (seq, own_mix_ref, own_ref)):
            own = normed_ref[pl.ds(pl.multiple_of(place * rows, rows), rows), :].astype(F32)
            mixed = own + jnp.dot(mix_ref[...], normed_ref[...], preferred_element_type=F32)
            out_ref[member] = mixed.astype(BF16)


def mix(seq, parts, own_mix, mate_mix):
    group, _, inner = parts[0].shape
    rows, total = own_mix.shape
    return pl.pallas_call(
        mix_kernel,
        in_specs=[SMEM] + [VMEM] * (len(parts) + 2),
        out_specs=[VMEM] * 2,
        out_shape=[jax.ShapeDtypeStruct((group, rows, inner), BF16)] * 2,
        scratch_shapes=[pltpu.VMEM((total, inner), BF16)],
        compiler_params=params(12),
        cost_estimate=pl.CostEstimate(
            flops=4 * group * total * inner * rows,
            bytes_accessed=2 * total * (group * inner * len(parts) + 2 * rows),
            transcendentals=total,
        ),
    )(seq, *parts, own_mix, mate_mix)


def tail_kernel(shares, count, seq_ref, *refs):
    pieces, refs = refs[:count], refs[count:]
    cand_ref, w_gate_ref, w_out_ref = refs[:3]
    ups, downs = refs[3 : 3 + shares], refs[3 + shares : 3 + 2 * shares]
    out_ref, mixed_ref = refs[3 + 2 * shares :]
    users, rows, width = cand_ref.shape
    inner = w_gate_ref.shape[1]
    if count == 1:
        mixed_ref[...] = pieces[0][...]
    else:
        group = pieces[0].shape[0]
        odd = seq_ref[0] & 1
        for k, piece in enumerate(pieces):
            for member in range(group):
                mixed_ref[(odd ^ 1 ^ k) * group + member] = piece[member]
    cand = cand_ref[...].reshape(users * rows, width)
    gate = silu(jnp.dot(cand, w_gate_ref[...], preferred_element_type=F32))
    gated = (mixed_ref[...].reshape(users * rows, inner).astype(F32) * gate).astype(BF16)
    state = cand.astype(F32) + jnp.dot(gated, w_out_ref[...], preferred_element_type=F32)
    ffn_in = layer_norm(state).astype(BF16)
    total = state
    for up, down in zip(ups, downs):
        hidden = gelu(jnp.dot(ffn_in, up[...], preferred_element_type=F32)).astype(BF16)
        total = total + jnp.dot(hidden, down[...], preferred_element_type=F32)
    out_ref[...] = total.astype(BF16).reshape(users, rows, width)


def tail(seq, pieces, candidates, w_gate, w_out, ups, downs):
    users, rows, width = candidates.shape
    inner = w_gate.shape[1]
    hidden = sum(up.shape[1] for up in ups)
    total = users * rows
    return pl.pallas_call(
        functools.partial(tail_kernel, len(ups), len(pieces)),
        in_specs=[SMEM] + [VMEM] * (len(pieces) + 3 + 2 * len(ups)),
        out_specs=VMEM,
        out_shape=jax.ShapeDtypeStruct((users, rows, width), BF16),
        scratch_shapes=[pltpu.VMEM((users, rows, inner), BF16)],
        compiler_params=params(24),
        cost_estimate=pl.CostEstimate(
            flops=2 * total * width * (2 * inner + 2 * hidden),
            bytes_accessed=2 * width * (2 * hidden + inner + 2 * total),
            transcendentals=total * hidden,
        ),
    )(seq, *pieces, candidates, w_gate, w_out, *ups, *downs)


def narrow_exchanges(share, count):
    held = [share]
    step = count // 4
    while step:
        held = held + [lax.ppermute(a, "usr", [(i, i ^ step) for i in range(count)]) for a in held]
        step //= 2
    return held[1:]


def together(*values):
    return lax.optimization_barrier(values)


def mixed_by_pairs(seq, queries, later, history_kv, lengths, token_mix, own, first_wide, second_wide):
    count = 4
    mate, cross = [[(i, i ^ k) for i in range(count)] for k in (1, 2)]
    attend = functools.partial(attention, seq, lengths, history_kv=history_kv, total=2 * queries.shape[1])

    crossed = lax.ppermute(queries, "seq", cross)
    mated = lax.ppermute(queries, "seq", mate)
    give_own, keep_own = attend([later], [0], sides=(0, 1))
    give_own, keep_own = attend([mated], [1], sides=(0, 1), into=[give_own, keep_own])
    crossed, give_own, keep_own, own, token_mix = together(crossed, give_own, keep_own, own, token_mix)
    opposite = lax.ppermute(crossed, "seq", mate)
    given_own = lax.ppermute(give_own, "seq", mate)
    give_other, keep_other = attend([crossed], [0], sides=(0, 1))
    opposite, first_wide = together(opposite, first_wide)
    second_wide = second_wide(own)
    give_other = attend([opposite], [1], sides=(0,), into=[give_other])[0]
    give_other, keep_other = together(give_other, keep_other)
    given_other = lax.ppermute(give_other, "seq", mate)
    keep_other = attend([opposite], [1], sides=(1,), into=[keep_other])[0]

    keep_own = keep_own + given_own
    came_other = lax.ppermute(keep_own, "seq", cross)
    keep_other = keep_other + given_other
    came_own = lax.ppermute(keep_other, "seq", cross)

    mate_mix = lax.ppermute(token_mix, "seq", mate)
    mixed, mate_mixed = mix(seq, [keep_own, keep_other, came_own, came_other], token_mix, mate_mix)
    return [mixed, lax.ppermute(mate_mixed, "seq", mate)], own, [first_wide, second_wide]


def mixed_scattered(seq, queries, history_kv, lengths, token_mix):
    gathered = lax.all_gather(queries, "seq", axis=1, tiled=True)
    sums = attention(seq, lengths, [gathered], [None], history_kv, gathered.shape[1], (None,))[0]
    attended = lax.psum_scatter(sums.astype(F32), "seq", scatter_dimension=1, tiled=True)
    normed = layer_norm(attended).astype(BF16)
    everyone = lax.all_gather(normed, "seq", axis=1, tiled=True)
    mixed = normed.astype(F32) + jnp.einsum("cp,upe->uce", token_mix, everyone, preferred_element_type=F32)
    return [mixed.astype(BF16)]


def shards(seq_count, usr_count, history_kv, candidates, lengths, w_query, w_gate, token_mix, w_out, w_up, w_down):
    users, rows, width = candidates.shape
    inner = w_query.shape[1]
    seq = lax.axis_index("seq").astype(jnp.int32).reshape(1)
    flat = candidates.reshape(users * rows, width)
    queries = jnp.dot(flat, w_query, preferred_element_type=F32).astype(BF16).reshape(users, rows, inner)
    by_pairs = seq_count == 4 and users % 2 == 0
    doubled = usr_count & (usr_count - 1) == 0 and usr_count > 1
    later, weights = together(queries, [w_up, w_down])
    half = usr_count // 2
    widest = [(i, i ^ half) for i in range(usr_count)]
    if doubled:
        own = [[w] + narrow_exchanges(v, usr_count) for v, w in zip((w_up, w_down), weights)]
        wide = lax.ppermute(weights[0], "usr", widest)
    else:
        own = [[g[i] for i in range(usr_count)] for g in (lax.all_gather(w, "usr") for w in weights)]
        wide = w_up

    def second(own):
        return lax.ppermute(own[1][0], "usr", widest) if doubled else w_down

    if by_pairs:
        pieces, own, wide = mixed_by_pairs(seq, queries, later, history_kv, lengths, token_mix, own, wide, second)
    else:
        pieces = mixed_scattered(seq, later, history_kv, lengths, token_mix)
        wide = [wide, second(own)]
    shares = own
    if doubled:
        pieces[0], wide = together(pieces[0], wide)
        shares = [o + [b] + narrow_exchanges(b, usr_count) for o, b in zip(own, wide)]
    return tail(seq, pieces, candidates, w_gate, w_out, *shares)


def solution(mesh):
    return jax.shard_map(
        functools.partial(shards, mesh.shape["seq"], mesh.shape["usr"]),
        mesh=mesh,
        in_specs=(
            P(("grp", "usr"), "seq", None),
            P(("grp", "usr"), "seq", None),
            P(("grp", "usr")),
            P(),
            P(),
            P("seq", None),
            P(),
            P(None, "usr"),
            P("usr", None),
        ),
        out_specs=P(("grp", "usr"), "seq", None),
        check_vma=False,
    )
```

```python
import functools
import math

import jax
import jax.numpy as jnp
from jax import lax
from jax.experimental import pallas as pl
from jax.experimental.pallas import tpu as pltpu
from jax.sharding import PartitionSpec as P

HEADS = 3
DH = 128
EPS = 1e-05
F32 = jnp.float32
BF16 = jnp.bfloat16
WEIGHT = 3
VMEM = pl.BlockSpec(memory_space=pltpu.VMEM)
SMEM = pl.BlockSpec(memory_space=pltpu.SMEM)


def layer_norm(values):
    center = values - jnp.mean(values, axis=-1, keepdims=True)
    spread = jnp.mean(center * center, axis=-1, keepdims=True)
    return center * lax.rsqrt(spread + EPS)


def silu(values):
    half = 0.5 * values
    return half + half * jnp.tanh(half)


def gelu(values):
    scale = math.sqrt(2 / math.pi)
    half = 0.5 * values
    return half + half * jnp.tanh(values * (scale + (scale * 0.044715) * (values * values)))


def params(mib):
    return pltpu.CompilerParams(vmem_limit_bytes=mib * 1024 * 1024)


def attention_kernel(places, sides, seq_ref, lengths_ref, *refs):
    count = len(places)
    chunks, kv_ref = refs[:count], refs[count]
    outs = refs[-len(sides) :]
    _, rows, inner = chunks[0].shape
    slots = kv_ref.shape[1]
    half_scale = 0.5 / math.sqrt(DH)
    seq = seq_ref[0]
    odd = seq & 1
    block = math.gcd(rows, 128)
    for out_ref, side in zip(outs, sides):
        group = out_ref.shape[0]
        first = 0 if side is None else (odd ^ side) * group
        for member in range(group):
            user = first + member
            limit = lengths_ref[user] - seq * slots
            valid = lax.broadcasted_iota(jnp.int32, (slots, DH), 0) < limit
            heads = [slice(h * DH, (h + 1) * DH) for h in range(inner // DH)]
            values = [
                jnp.where(valid, kv_ref[user, :, inner + c.start : inner + c.stop], jnp.zeros((), BF16)) for c in heads
            ]
            for j, chunk in enumerate(chunks):
                for r in range(0, rows, block):
                    halves = [
                        half_scale
                        * lax.dot_general(
                            chunk[user, r : r + block, c],
                            kv_ref[user, :, c],
                            (((1,), (1,)), ((), ())),
                            preferred_element_type=F32,
                        )
                        for c in heads
                    ]
                    weights = [(half + half * jnp.tanh(half)).astype(BF16) for half in halves]
                    sums = [jnp.dot(w, v, preferred_element_type=F32).astype(BF16) for w, v in zip(weights, values)]
                    start = r if places[j] is None else pl.multiple_of((odd ^ places[j]) * rows + r, block)
                    out_ref[member, pl.ds(start, block), :] = jnp.concatenate(sums, axis=1)


def attention(seq, lengths, chunks, places, history_kv, total, sides, into=()):
    count = len(chunks)
    users, rows, inner = chunks[0].shape
    slots, width = history_kv.shape[1:]
    group = users if sides[0] is None else users // 2
    work = group * len(sides) * rows * count * slots * inner
    return pl.pallas_call(
        functools.partial(attention_kernel, places, sides),
        in_specs=[SMEM, SMEM] + [VMEM] * (count + 1 + len(into)),
        out_specs=[VMEM] * len(sides),
        out_shape=[jax.ShapeDtypeStruct((group, total, inner), BF16)] * len(sides),
        input_output_aliases={3 + count + i: i for i in range(len(into))},
        compiler_params=params(16),
        cost_estimate=pl.CostEstimate(
            flops=WEIGHT * 4 * work, bytes_accessed=2 * users * (slots * width + 2 * rows * count * inner), transcendentals=work // DH
        ),
    )(seq, lengths, *chunks, history_kv, *into)


def mix_kernel(seq_ref, *refs):
    parts, (own_mix_ref, mate_mix_ref, own_ref, mate_ref, normed_ref) = refs[:-5], refs[-5:]
    seq = seq_ref[0]
    pair = seq >> 1
    half = parts[0].shape[1]
    rows = half // 2
    for member in range(parts[0].shape[0]):
        for k in range(2):
            attended = sum(p[member].astype(F32) for p in parts[k::2])
            start = pl.multiple_of((pair ^ k) * half, half)
            normed_ref[pl.ds(start, half), :] = layer_norm(attended).astype(BF16)
        for place, mix_ref, out_ref in ((seq ^ 1, mate_mix_ref, mate_ref), (seq, own_mix_ref, own_ref)):
            own = normed_ref[pl.ds(pl.multiple_of(place * rows, rows), rows), :].astype(F32)
            mixed = own + jnp.dot(mix_ref[...], normed_ref[...], preferred_element_type=F32)
            out_ref[member] = mixed.astype(BF16)


def mix(seq, parts, own_mix, mate_mix):
    group, _, inner = parts[0].shape
    rows, total = own_mix.shape
    return pl.pallas_call(
        mix_kernel,
        in_specs=[SMEM] + [VMEM] * (len(parts) + 2),
        out_specs=[VMEM] * 2,
        out_shape=[jax.ShapeDtypeStruct((group, rows, inner), BF16)] * 2,
        scratch_shapes=[pltpu.VMEM((total, inner), BF16)],
        compiler_params=params(12),
        cost_estimate=pl.CostEstimate(
            flops=4 * group * total * inner * rows,
            bytes_accessed=2 * total * (group * inner * len(parts) + 2 * rows),
            transcendentals=total,
        ),
    )(seq, *parts, own_mix, mate_mix)


def tail_kernel(shares, side, seq_ref, mixed_ref, cand_ref, w_gate_ref, w_out_ref, *refs):
    ups, downs = refs[:shares], refs[shares : 2 * shares]
    done, out_ref = refs[2 * shares : -1], refs[-1]
    group, rows, inner = mixed_ref.shape
    odd = seq_ref[0] & 1
    first = 0 if side is None else (odd ^ side) * group
    cand = jnp.concatenate([cand_ref[first + member] for member in range(group)], axis=0)
    gate = silu(jnp.dot(cand, w_gate_ref[...], preferred_element_type=F32))
    gated = (mixed_ref[...].reshape(group * rows, inner).astype(F32) * gate).astype(BF16)
    state = cand.astype(F32) + jnp.dot(gated, w_out_ref[...], preferred_element_type=F32)
    ffn_in = layer_norm(state).astype(BF16)
    total = state
    for up, down in zip(ups, downs):
        hidden = gelu(jnp.dot(ffn_in, up[...], preferred_element_type=F32)).astype(BF16)
        total = total + jnp.dot(hidden, down[...], preferred_element_type=F32)
    total = total.astype(BF16)
    if not done:
        out_ref[...] = total.reshape(out_ref.shape)
        return
    for member in range(group):
        out_ref[first + member] = total[member * rows : (member + 1) * rows]
        out_ref[(odd ^ side ^ 1) * group + member] = done[0][member]


def tail(seq, mixed, side, candidates, w_gate, w_out, ups, downs, done=()):
    users, rows, width = candidates.shape
    group, _, inner = mixed.shape
    hidden = sum(up.shape[1] for up in ups)
    total = group * rows
    return pl.pallas_call(
        functools.partial(tail_kernel, len(ups), side),
        in_specs=[SMEM] + [VMEM] * (4 + 2 * len(ups) + len(done)),
        out_specs=VMEM,
        out_shape=jax.ShapeDtypeStruct((users if done else group, rows, width), BF16),
        compiler_params=params(24),
        cost_estimate=pl.CostEstimate(
            flops=2 * total * width * (2 * inner + 2 * hidden),
            bytes_accessed=2 * width * (2 * hidden + inner + 2 * total),
            transcendentals=total * hidden,
        ),
    )(seq, mixed, candidates, w_gate, w_out, *ups, *downs, *done)


def narrow_exchanges(share, count):
    held = [share]
    step = count // 4
    while step:
        held = held + [lax.ppermute(a, "usr", [(i, i ^ step) for i in range(count)]) for a in held]
        step //= 2
    return held[1:]


def together(*values):
    return lax.optimization_barrier(values)


def mixed_by_pairs(seq, queries, later, history_kv, lengths, token_mix, own, first_wide, second_wide):
    count = 4
    mate, cross = [[(i, i ^ k) for i in range(count)] for k in (1, 2)]
    attend = functools.partial(attention, seq, lengths, history_kv=history_kv, total=2 * queries.shape[1])

    crossed = lax.ppermute(queries, "seq", cross)
    mated = lax.ppermute(queries, "seq", mate)
    give_own, keep_own = attend([later], [0], sides=(0, 1))
    give_own, keep_own = attend([mated], [1], sides=(0, 1), into=[give_own, keep_own])
    crossed, give_own, keep_own, own, token_mix = together(crossed, give_own, keep_own, own, token_mix)
    opposite = lax.ppermute(crossed, "seq", mate)
    given_own = lax.ppermute(give_own, "seq", mate)
    give_other, keep_other = attend([crossed], [0], sides=(0, 1))
    opposite, first_wide = together(opposite, first_wide)
    second_wide = second_wide(own)
    give_other = attend([opposite], [1], sides=(0,), into=[give_other])[0]
    give_other, keep_other = together(give_other, keep_other)
    given_other = lax.ppermute(give_other, "seq", mate)
    keep_other = attend([opposite], [1], sides=(1,), into=[keep_other])[0]

    keep_own = keep_own + given_own
    came_other = lax.ppermute(keep_own, "seq", cross)
    keep_other = keep_other + given_other
    came_own = lax.ppermute(keep_other, "seq", cross)

    mate_mix = lax.ppermute(token_mix, "seq", mate)
    mixed, mate_mixed = mix(seq, [keep_own, keep_other, came_own, came_other], token_mix, mate_mix)
    return [mixed, lax.ppermute(mate_mixed, "seq", mate)], own, [first_wide, second_wide]


def mixed_scattered(seq, queries, history_kv, lengths, token_mix):
    gathered = lax.all_gather(queries, "seq", axis=1, tiled=True)
    sums = attention(seq, lengths, [gathered], [None], history_kv, gathered.shape[1], (None,))[0]
    attended = lax.psum_scatter(sums.astype(F32), "seq", scatter_dimension=1, tiled=True)
    normed = layer_norm(attended).astype(BF16)
    everyone = lax.all_gather(normed, "seq", axis=1, tiled=True)
    mixed = normed.astype(F32) + jnp.einsum("cp,upe->uce", token_mix, everyone, preferred_element_type=F32)
    return [mixed.astype(BF16)]


def shards(seq_count, usr_count, history_kv, candidates, lengths, w_query, w_gate, token_mix, w_out, w_up, w_down):
    users, rows, width = candidates.shape
    inner = w_query.shape[1]
    seq = lax.axis_index("seq").astype(jnp.int32).reshape(1)
    flat = candidates.reshape(users * rows, width)
    queries = jnp.dot(flat, w_query, preferred_element_type=F32).astype(BF16).reshape(users, rows, inner)
    by_pairs = seq_count == 4 and users % 2 == 0
    doubled = usr_count & (usr_count - 1) == 0 and usr_count > 1
    later, weights = together(queries, [w_up, w_down])
    half = usr_count // 2
    widest = [(i, i ^ half) for i in range(usr_count)]
    if doubled:
        own = [[w] + narrow_exchanges(v, usr_count) for v, w in zip((w_up, w_down), weights)]
        wide = lax.ppermute(weights[0], "usr", widest)
    else:
        own = [[g[i] for i in range(usr_count)] for g in (lax.all_gather(w, "usr") for w in weights)]
        wide = w_up

    def second(own):
        return lax.ppermute(own[1][0], "usr", widest) if doubled else w_down

    if by_pairs:
        pieces, own, wide = mixed_by_pairs(seq, queries, later, history_kv, lengths, token_mix, own, wide, second)
    else:
        pieces = mixed_scattered(seq, later, history_kv, lengths, token_mix)
        wide = [wide, second(own)]
    shares = own
    if doubled:
        pieces[0], wide = together(pieces[0], wide)
        shares = [o + [b] + narrow_exchanges(b, usr_count) for o, b in zip(own, wide)]
    finish = functools.partial(tail, seq, candidates=candidates, w_gate=w_gate, w_out=w_out, ups=shares[0], downs=shares[1])
    if not by_pairs:
        return finish(pieces[0], None)
    kept = finish(pieces[0], 1)
    return finish(pieces[1], 0, done=[kept])


def solution(mesh):
    return jax.shard_map(
        functools.partial(shards, mesh.shape["seq"], mesh.shape["usr"]),
        mesh=mesh,
        in_specs=(
            P(("grp", "usr"), "seq", None),
            P(("grp", "usr"), "seq", None),
            P(("grp", "usr")),
            P(),
            P(),
            P("seq", None),
            P(),
            P(None, "usr"),
            P("usr", None),
        ),
        out_specs=P(("grp", "usr"), "seq", None),
        check_vma=False,
    )
```

```python
import functools
import math

import jax
import jax.numpy as jnp
from jax import lax
from jax.experimental import pallas as pl
from jax.experimental.pallas import tpu as pltpu
from jax.sharding import PartitionSpec as P

HEADS = 3
DH = 128
EPS = 1e-05
F32 = jnp.float32
BF16 = jnp.bfloat16
WEIGHT = 3
VMEM = pl.BlockSpec(memory_space=pltpu.VMEM)
SMEM = pl.BlockSpec(memory_space=pltpu.SMEM)


def layer_norm(values):
    center = values - jnp.mean(values, axis=-1, keepdims=True)
    spread = jnp.mean(center * center, axis=-1, keepdims=True)
    return center * lax.rsqrt(spread + EPS)


def silu(values):
    half = 0.5 * values
    return half + half * jnp.tanh(half)


def gelu(values):
    scale = math.sqrt(2 / math.pi)
    half = 0.5 * values
    return half + half * jnp.tanh(values * (scale + (scale * 0.044715) * (values * values)))


def params(mib):
    return pltpu.CompilerParams(vmem_limit_bytes=mib * 1024 * 1024)


def attention_kernel(places, sides, seq_ref, lengths_ref, *refs):
    count = len(places)
    chunks, kv_ref = refs[:count], refs[count]
    outs = refs[-len(sides) :]
    _, rows, inner = chunks[0].shape
    slots = kv_ref.shape[1]
    half_scale = 0.5 / math.sqrt(DH)
    seq = seq_ref[0]
    odd = seq & 1
    block = math.gcd(rows, 128)
    for out_ref, side in zip(outs, sides):
        group = out_ref.shape[0]
        first = 0 if side is None else (odd ^ side) * group
        for member in range(group):
            user = first + member
            limit = lengths_ref[user] - seq * slots
            valid = lax.broadcasted_iota(jnp.int32, (slots, DH), 0) < limit
            heads = [slice(h * DH, (h + 1) * DH) for h in range(inner // DH)]
            values = [
                jnp.where(valid, kv_ref[user, :, inner + c.start : inner + c.stop], jnp.zeros((), BF16)) for c in heads
            ]
            for j, chunk in enumerate(chunks):
                for r in range(0, rows, block):
                    halves = [
                        half_scale
                        * lax.dot_general(
                            chunk[user, r : r + block, c],
                            kv_ref[user, :, c],
                            (((1,), (1,)), ((), ())),
                            preferred_element_type=F32,
                        )
                        for c in heads
                    ]
                    weights = [(half + half * jnp.tanh(half)).astype(BF16) for half in halves]
                    sums = [jnp.dot(w, v, preferred_element_type=F32).astype(BF16) for w, v in zip(weights, values)]
                    start = r if places[j] is None else pl.multiple_of((odd ^ places[j]) * rows + r, block)
                    out_ref[member, pl.ds(start, block), :] = jnp.concatenate(sums, axis=1)


def attention(seq, lengths, chunks, places, history_kv, total, sides, into=()):
    count = len(chunks)
    users, rows, inner = chunks[0].shape
    slots, width = history_kv.shape[1:]
    group = users if sides[0] is None else users // 2
    work = group * len(sides) * rows * count * slots * inner
    return pl.pallas_call(
        functools.partial(attention_kernel, places, sides),
        in_specs=[SMEM, SMEM] + [VMEM] * (count + 1 + len(into)),
        out_specs=[VMEM] * len(sides),
        out_shape=[jax.ShapeDtypeStruct((group, total, inner), BF16)] * len(sides),
        input_output_aliases={3 + count + i: i for i in range(len(into))},
        compiler_params=params(16),
        cost_estimate=pl.CostEstimate(
            flops=WEIGHT * 4 * work, bytes_accessed=2 * users * (slots * width + 2 * rows * count * inner), transcendentals=work // DH
        ),
    )(seq, lengths, *chunks, history_kv, *into)


def mix_kernel(seq_ref, *refs):
    parts, (own_mix_ref, mate_mix_ref, own_ref, mate_ref, normed_ref) = refs[:-5], refs[-5:]
    seq = seq_ref[0]
    pair = seq >> 1
    half = parts[0].shape[1]
    rows = half // 2
    for member in range(parts[0].shape[0]):
        for k in range(2):
            attended = sum(p[member].astype(F32) for p in parts[k::2])
            start = pl.multiple_of((pair ^ k) * half, half)
            normed_ref[pl.ds(start, half), :] = layer_norm(attended).astype(BF16)
        for place, mix_ref, out_ref in ((seq ^ 1, mate_mix_ref, mate_ref), (seq, own_mix_ref, own_ref)):
            own = normed_ref[pl.ds(pl.multiple_of(place * rows, rows), rows), :].astype(F32)
            mixed = own + jnp.dot(mix_ref[...], normed_ref[...], preferred_element_type=F32)
            out_ref[member] = mixed.astype(BF16)


def mix(seq, parts, own_mix, mate_mix):
    group, _, inner = parts[0].shape
    rows, total = own_mix.shape
    return pl.pallas_call(
        mix_kernel,
        in_specs=[SMEM] + [VMEM] * (len(parts) + 2),
        out_specs=[VMEM] * 2,
        out_shape=[jax.ShapeDtypeStruct((group, rows, inner), BF16)] * 2,
        scratch_shapes=[pltpu.VMEM((total, inner), BF16)],
        compiler_params=params(12),
        cost_estimate=pl.CostEstimate(
            flops=4 * group * total * inner * rows,
            bytes_accessed=2 * total * (group * inner * len(parts) + 2 * rows),
            transcendentals=total,
        ),
    )(seq, *parts, own_mix, mate_mix)


def tail_kernel(shares, side, seq_ref, mixed_ref, cand_ref, w_gate_ref, w_out_ref, *refs):
    ups, downs = refs[:shares], refs[shares : 2 * shares]
    later = len(refs) > 2 * shares + 1
    if later:
        done_ref, out_ref, held_ref, sems = refs[2 * shares :]
    else:
        out_ref = refs[-1]
    group, rows, inner = mixed_ref.shape
    odd = seq_ref[0] & 1
    first = 0 if side is None else (odd ^ side) * group
    copies = []
    if later:
        copies.append(pltpu.make_async_copy(done_ref, out_ref.at[pl.ds((odd ^ side ^ 1) * group, group)], sems.at[0]))
        copies[0].start()
    cand = jnp.concatenate([cand_ref[first + member] for member in range(group)], axis=0)
    gate = silu(jnp.dot(cand, w_gate_ref[...], preferred_element_type=F32))
    gated = (mixed_ref[...].reshape(group * rows, inner).astype(F32) * gate).astype(BF16)
    state = cand.astype(F32) + jnp.dot(gated, w_out_ref[...], preferred_element_type=F32)
    ffn_in = layer_norm(state).astype(BF16)
    hidden = [gelu(jnp.dot(ffn_in, up[...], preferred_element_type=F32)).astype(BF16) for up in ups]
    width = state.shape[1]
    cut = width // 256 * 128 or width
    for k, start in enumerate(range(0, width, cut)):
        cols = pl.ds(start, min(cut, width - start))
        total = state[:, start : start + cut]
        for h, down in zip(hidden, downs):
            total = total + jnp.dot(h, down[:, cols], preferred_element_type=F32)
        total = total.astype(BF16).reshape(group, rows, -1)
        if not later:
            out_ref[:, :, cols] = total
            continue
        held_ref[:, :, cols] = total
        target = out_ref.at[pl.ds(first, group), :, cols]
        copies.append(pltpu.make_async_copy(held_ref.at[:, :, cols], target, sems.at[k + 1]))
        copies[-1].start()
    for copy in copies:
        copy.wait()


def tail(seq, mixed, side, candidates, w_gate, w_out, ups, downs, done=()):
    users, rows, width = candidates.shape
    group, _, inner = mixed.shape
    hidden = sum(up.shape[1] for up in ups)
    total = group * rows
    return pl.pallas_call(
        functools.partial(tail_kernel, len(ups), side),
        in_specs=[SMEM] + [VMEM] * (4 + 2 * len(ups) + len(done)),
        out_specs=pl.BlockSpec(memory_space=pl.ANY) if done else VMEM,
        out_shape=jax.ShapeDtypeStruct((users if done else group, rows, width), BF16),
        scratch_shapes=[pltpu.VMEM((group, rows, width), BF16), pltpu.SemaphoreType.DMA((4,))] if done else [],
        compiler_params=params(24),
        cost_estimate=pl.CostEstimate(
            flops=2 * total * width * (2 * inner + 2 * hidden),
            bytes_accessed=2 * width * (2 * hidden + inner + 2 * total),
            transcendentals=total * hidden,
        ),
    )(seq, mixed, candidates, w_gate, w_out, *ups, *downs, *done)


def narrow_exchanges(share, count):
    held = [share]
    step = count // 4
    while step:
        held = held + [lax.ppermute(a, "usr", [(i, i ^ step) for i in range(count)]) for a in held]
        step //= 2
    return held[1:]


def together(*values):
    return lax.optimization_barrier(values)


def mixed_by_pairs(seq, queries, later, history_kv, lengths, token_mix, own, first_wide, second_wide):
    count = 4
    mate, cross = [[(i, i ^ k) for i in range(count)] for k in (1, 2)]
    attend = functools.partial(attention, seq, lengths, history_kv=history_kv, total=2 * queries.shape[1])

    crossed = lax.ppermute(queries, "seq", cross)
    mated = lax.ppermute(queries, "seq", mate)
    give_own, keep_own = attend([later], [0], sides=(0, 1))
    give_own, keep_own = attend([mated], [1], sides=(0, 1), into=[give_own, keep_own])
    crossed, give_own, keep_own, own, token_mix = together(crossed, give_own, keep_own, own, token_mix)
    opposite = lax.ppermute(crossed, "seq", mate)
    given_own = lax.ppermute(give_own, "seq", mate)
    give_other, keep_other = attend([crossed], [0], sides=(0, 1))
    opposite, first_wide = together(opposite, first_wide)
    second_wide = second_wide(own)
    give_other = attend([opposite], [1], sides=(0,), into=[give_other])[0]
    give_other, keep_other = together(give_other, keep_other)
    given_other = lax.ppermute(give_other, "seq", mate)
    keep_other = attend([opposite], [1], sides=(1,), into=[keep_other])[0]

    keep_own = keep_own + given_own
    came_other = lax.ppermute(keep_own, "seq", cross)
    keep_other = keep_other + given_other
    came_own = lax.ppermute(keep_other, "seq", cross)

    mate_mix = lax.ppermute(token_mix, "seq", mate)
    mixed, mate_mixed = mix(seq, [keep_own, keep_other, came_own, came_other], token_mix, mate_mix)
    return [mixed, lax.ppermute(mate_mixed, "seq", mate)], own, [first_wide, second_wide]


def mixed_scattered(seq, queries, history_kv, lengths, token_mix):
    gathered = lax.all_gather(queries, "seq", axis=1, tiled=True)
    sums = attention(seq, lengths, [gathered], [None], history_kv, gathered.shape[1], (None,))[0]
    attended = lax.psum_scatter(sums.astype(F32), "seq", scatter_dimension=1, tiled=True)
    normed = layer_norm(attended).astype(BF16)
    everyone = lax.all_gather(normed, "seq", axis=1, tiled=True)
    mixed = normed.astype(F32) + jnp.einsum("cp,upe->uce", token_mix, everyone, preferred_element_type=F32)
    return [mixed.astype(BF16)]


def shards(seq_count, usr_count, history_kv, candidates, lengths, w_query, w_gate, token_mix, w_out, w_up, w_down):
    users, rows, width = candidates.shape
    inner = w_query.shape[1]
    seq = lax.axis_index("seq").astype(jnp.int32).reshape(1)
    flat = candidates.reshape(users * rows, width)
    queries = jnp.dot(flat, w_query, preferred_element_type=F32).astype(BF16).reshape(users, rows, inner)
    by_pairs = seq_count == 4 and users % 2 == 0
    doubled = usr_count & (usr_count - 1) == 0 and usr_count > 1
    later, weights = together(queries, [w_up, w_down])
    half = usr_count // 2
    widest = [(i, i ^ half) for i in range(usr_count)]
    if doubled:
        own = [[w] + narrow_exchanges(v, usr_count) for v, w in zip((w_up, w_down), weights)]
        wide = lax.ppermute(weights[0], "usr", widest)
    else:
        own = [[g[i] for i in range(usr_count)] for g in (lax.all_gather(w, "usr") for w in weights)]
        wide = w_up

    def second(own):
        return lax.ppermute(own[1][0], "usr", widest) if doubled else w_down

    if by_pairs:
        pieces, own, wide = mixed_by_pairs(seq, queries, later, history_kv, lengths, token_mix, own, wide, second)
    else:
        pieces = mixed_scattered(seq, later, history_kv, lengths, token_mix)
        wide = [wide, second(own)]
    shares = own
    if doubled:
        pieces[0], wide = together(pieces[0], wide)
        shares = [o + [b] + narrow_exchanges(b, usr_count) for o, b in zip(own, wide)]
    finish = functools.partial(tail, seq, candidates=candidates, w_gate=w_gate, w_out=w_out, ups=shares[0], downs=shares[1])
    if not by_pairs:
        return finish(pieces[0], None)
    kept = finish(pieces[0], 1)
    return finish(pieces[1], 0, done=[kept])


def solution(mesh):
    return jax.shard_map(
        functools.partial(shards, mesh.shape["seq"], mesh.shape["usr"]),
        mesh=mesh,
        in_specs=(
            P(("grp", "usr"), "seq", None),
            P(("grp", "usr"), "seq", None),
            P(("grp", "usr")),
            P(),
            P(),
            P("seq", None),
            P(),
            P(None, "usr"),
            P("usr", None),
        ),
        out_specs=P(("grp", "usr"), "seq", None),
        check_vma=False,
    )
```
